256 devices in a mesh: wide: 16 (over y, z_hi, core), node: 16 (over z_lo, x).
Axes of the slice: x: 4, y: 4, z: 8 (z_hi: 2, z_lo: 4; z = z_hi * 4 + z_lo), core: 2. Of those that a mesh axis runs over, the one named last changes fastest.
Arguments:
- grad_codes: int32 [16, 16, 128, 9216], P('wide', 'node'), may hold values from -8 to 7
- scales: float32 [16, 16, 128, 72], P('wide', 'node'), may hold values from 0.01 to 0.2
- feedback: bfloat16 [16, 16, 128, 9216], P('wide', 'node'), may hold values from -1.1953125 to 1.1953125
- master: float32 [16, 16, 4608], P('node', 'wide'), may hold values from -0.3 to 0.3
- moment: float32 [16, 16, 4608], P('node', 'wide'), may hold values from -0.006 to 0.006
- second: float32 [16, 16, 4608], P('node', 'wide'), may hold values from 4e-06 to 0.0001
Outputs:
- adam_dir: float32 [16, 16, 4608], P('node', 'wide')
- new_master: float32 [16, 16, 4608], P('node', 'wide')
- weights_bf16: bfloat16 [128, 9216], replicated
The draws below stay inside these ranges and needn't reach their ends.
Inputs may be any that keep to these rules, and one draw needn't show every extreme that they name: `grad_codes`: int4 codes.
All inputs are finite; a program needn't handle non-finite values.
Results may differ from the reference program's by a relative error of at most 0.018.
Values may be sent and summed in bfloat16 or wider, within the bound.
No kernel may reach another device: no remote copies, remote signals or barrier semaphores. Data moves between devices by JAX's collectives and lax.ppermute only.
A program may use at most 64 MiB of HBM per device.

```python
import math
import jax
import jax.numpy as jnp
from jax import lax

D = 9216
BLOCK = 128
GROWS = 128
SLAB = 4608
N_WIDE = 16
N_NODE = 16


def place_ends(entries, rng, low, high):
    longest = entries.shape.index(max(entries.shape))
    spots = []
    for shift in (0, 1):
        where = [jax.random.randint(jax.random.fold_in(rng, axis), (), 0, length) for axis, length in enumerate(entries.shape)]
        where[longest] = (where[longest] + shift) % entries.shape[longest]
        spots.append(tuple(where))
    return entries.at[spots[0]].set(low).at[spots[1]].set(high)


def steps_of(own_key, extent, shards, least, largest):
    level, own = 1.0, jax.random.fold_in(own_key, 6)
    for position, shards_of in shards:
        draws = jnp.exp(jax.random.uniform(jax.random.fold_in(own, position), (shards_of,), jnp.float32, least / len(shards), largest / len(shards)))
        level = level * jnp.repeat(draws, extent[position] // shards_of).reshape([-1 if axis == position else 1 for axis in range(len(extent))])
    return level


def scatter_about(rng, shape, spread, reach, cuts=(), held_as=jnp.bfloat16):
    drawn = spread * jax.random.normal(rng, shape, jnp.float32)
    if cuts:
        drawn = drawn * steps_of(rng, shape, cuts, -0.22, 0.18)
    return jnp.clip(drawn, -reach, reach).astype(held_as)


def setup_inputs(seed: int = 0) -> dict:
    streams_of = jax.random.split(jax.random.key(seed), 7)
    grad_codes = place_ends(jax.random.randint(streams_of[0], (N_WIDE, N_NODE, GROWS, D), -8, 8), jax.random.fold_in(streams_of[0], 1), -8, 7).astype(jnp.int32)
    scales = jnp.clip(jnp.exp(math.log(0.2) - 2.9957323 * jax.random.uniform(streams_of[1], (N_WIDE, N_NODE, GROWS, D // BLOCK), jnp.float32) ** steps_of(streams_of[1], (N_WIDE, N_NODE, GROWS, D // BLOCK), ((0, 16), (1, 16)), -0.2, 0.2)), 0.01, 0.2)
    feedback = scatter_about(streams_of[2], (N_WIDE, N_NODE, GROWS, D), 0.2, 1.1953125, ((0, 16), (1, 16)))
    master = scatter_about(streams_of[3], (N_NODE, N_WIDE, SLAB), 0.05, 0.3, ((0, 16), (1, 16)), jnp.float32)
    moment = scatter_about(streams_of[4], (N_NODE, N_WIDE, SLAB), 0.001, 0.006, ((0, 16), (1, 16)), jnp.float32)
    second = jnp.clip(jnp.exp(math.log(0.0001) - 3.218876 * jax.random.uniform(streams_of[5], (N_NODE, N_WIDE, SLAB), jnp.float32) ** steps_of(streams_of[5], (N_NODE, N_WIDE, SLAB), ((0, 16), (1, 16)), -0.2, 0.2)), 3.999999989900971e-06, 0.0001)
    return dict(grad_codes=grad_codes, scales=scales, feedback=feedback, master=master, moment=moment, second=second)


beta_one = 0.9
beta_two = 0.999
adam_count = 100.0
adam_epsilon = 1e-08
learn_rate = 0.02

def reference(grad_codes, scales, feedback, master, moment, second):

    def wide_term(summed, inputs):
        codes_row, scales_row, feed_row = inputs
        dequant = codes_row.astype(jnp.float32).reshape(N_NODE, GROWS, D // BLOCK, BLOCK) * scales_row[..., None]
        compensated = (dequant.reshape(N_NODE, GROWS, D) + feed_row.astype(jnp.float32)).astype(jnp.bfloat16)
        pieces = compensated.reshape(N_NODE, N_NODE, N_WIDE, SLAB)
        node_sum = lax.optimization_barrier(jnp.sum(pieces.astype(jnp.float32), axis=0)).astype(jnp.bfloat16)
        return (summed + node_sum.astype(jnp.float32), None)
    start = jnp.zeros((N_NODE, N_WIDE, SLAB), jnp.float32)
    summed, unused = lax.scan(wide_term, start, (grad_codes, scales, feedback))
    grad = summed / (N_WIDE * N_NODE)
    first = beta_one * moment + (1.0 - beta_one) * grad
    squared = beta_two * second + (1.0 - beta_two) * grad * grad
    first_hat = first / (1.0 - beta_one ** adam_count)
    squared_hat = squared / (1.0 - beta_two ** adam_count)
    adam_dir = first_hat / (jnp.sqrt(squared_hat) + adam_epsilon)
    new_master = master - learn_rate * adam_dir
    weights_bf16 = new_master.astype(jnp.bfloat16).reshape(GROWS, D)
    return (adam_dir, new_master, weights_bf16)
```

```python
import functools

import jax
import jax.numpy as jnp
from jax import lax
from jax.experimental import pallas as pl
from jax.experimental.pallas import tpu as pltpu
from jax.sharding import Mesh
from jax.sharding import PartitionSpec as P

beta_one = 0.9
beta_two = 0.999
adam_count = 100.0
adam_epsilon = 1e-08
learn_rate = 0.02

AXES = ("y", "zh", "core", "zl", "x")
SIZES = (4, 2, 2, 4, 4)
ROWS = 128
WIDTH = 9216
HALF = WIDTH // 2
LANES = 128
CHUNKS = 4
CHUNK = HALF // CHUNKS
PER_CHUNK = CHUNK // LANES
SLAB_ROWS = HALF // LANES
F32 = jnp.float32
BF16 = jnp.bfloat16
VMEM = 48 * 1024 * 1024


def params():
    return pltpu.CompilerParams(vmem_limit_bytes=VMEM)


def owner_order(transposed):
    sent = lax.broadcasted_iota(jnp.int32, (ROWS, ROWS), 1 if transposed else 0)
    flat = lax.broadcasted_iota(jnp.int32, (ROWS, ROWS), 0 if transposed else 1)
    x, y, zl, zh = sent // 32, sent // 8 % 4, sent // 2 % 4, sent % 2
    return (zl * 32 + x * 8 + y * 2 + zh == flat).astype(F32).astype(BF16)


def compensate_kernel(half_ref, codes_ref, scales_ref, feedback_ref, out_ref, turned):
    first = (half_ref[0] * CHUNKS + pl.program_id(0)) * PER_CHUNK
    turned[0:PER_CHUNK, :] = scales_ref[pl.ds(first, PER_CHUNK), :]
    scale = turned[...].T
    for block in range(PER_CHUNK):
        columns = slice(block * LANES, (block + 1) * LANES)
        dequant = codes_ref[:, columns].astype(F32) * scale[:, block : block + 1]
        out_ref[:, columns] = (dequant + feedback_ref[:, columns].astype(F32)).astype(BF16)


def compensate(half, codes, scales, feedback):
    chunk = lambda i, half: (0, half[0] * CHUNKS + i)
    return pl.pallas_call(
        compensate_kernel,
        out_shape=jax.ShapeDtypeStruct((ROWS, HALF), BF16),
        grid_spec=pltpu.PrefetchScalarGridSpec(
            num_scalar_prefetch=1,
            grid=(CHUNKS,),
            in_specs=[
                pl.BlockSpec((ROWS, CHUNK), chunk),
                pl.BlockSpec((WIDTH // LANES, ROWS), lambda i, half: (0, 0)),
                pl.BlockSpec((ROWS, CHUNK), chunk),
            ],
            out_specs=pl.BlockSpec((ROWS, CHUNK), lambda i, half: (0, i)),
            scratch_shapes=[pltpu.VMEM((ROWS, LANES), F32)],
        ),
        compiler_params=params(),
        cost_estimate=pl.CostEstimate(flops=3 * ROWS * HALF, bytes_accessed=8 * ROWS * HALF, transcendentals=0),
        name="compensate",
    )(half, codes, scales, feedback)


def pair_sum_kernel(own_ref, other_ref, out_ref):
    order = owner_order(False)
    total = (own_ref[...].astype(F32) + other_ref[...].astype(F32)).astype(BF16)
    out_ref[...] = jnp.dot(order, total, preferred_element_type=F32).astype(BF16)


def pair_sum(own, other):
    block = pl.BlockSpec((ROWS, CHUNK), lambda i: (0, i))
    return pl.pallas_call(
        pair_sum_kernel,
        out_shape=jax.ShapeDtypeStruct((ROWS, HALF), BF16),
        grid=(CHUNKS,),
        in_specs=[block, block],
        out_specs=block,
        compiler_params=params(),
        name="pair_sum",
    )(own, other)


def plane_sum_kernel(in_ref, out_ref, spread):
    total = jnp.sum(in_ref[...].astype(F32), axis=0)
    for block in range(SLAB_ROWS):
        spread[:, block, :] = total[:, block * LANES : (block + 1) * LANES]
    out_ref[...] = spread[...].astype(BF16)


def plane_sum(arrived):
    return pl.pallas_call(
        plane_sum_kernel,
        out_shape=jax.ShapeDtypeStruct((8, SLAB_ROWS, LANES), BF16),
        scratch_shapes=[pltpu.VMEM((8, SLAB_ROWS, LANES), F32)],
        compiler_params=params(),
        name="plane_sum",
    )(arrived)


def adam_kernel(arrived_ref, master_ref, moment_ref, second_ref, dir_ref, new_ref, copies_ref):
    grad = jnp.sum(arrived_ref[...].astype(F32), axis=0) / 256.0
    first = beta_one * moment_ref[...] + (1.0 - beta_one) * grad
    squared = beta_two * second_ref[...] + (1.0 - beta_two) * grad * grad
    first_hat = first / (1.0 - beta_one**adam_count)
    squared_hat = squared / (1.0 - beta_two**adam_count)
    adam_dir = first_hat / (jnp.sqrt(squared_hat) + adam_epsilon)
    new_master = master_ref[...] - learn_rate * adam_dir
    dir_ref[...] = adam_dir
    new_ref[...] = new_master
    copies_ref[...] = jnp.broadcast_to(new_master.astype(BF16)[None], copies_ref.shape)


def adam(arrived, master, moment, second):
    slab = jax.ShapeDtypeStruct((SLAB_ROWS, LANES), F32)
    return pl.pallas_call(
        adam_kernel,
        out_shape=(slab, slab, jax.ShapeDtypeStruct((8, SLAB_ROWS, LANES), BF16)),
        compiler_params=params(),
        name="adam",
    )(arrived, master, moment, second)


def line_kernel(in_ref, out_ref, spread):
    spread[...] = in_ref[...].astype(F32)
    for block in range(SLAB_ROWS):
        columns = slice(block * LANES, (block + 1) * LANES)
        rows = spread[:, block, :].astype(BF16)
        out_ref[:, :, columns] = jnp.broadcast_to(rows[None], (16, 8, LANES))


def line_copies(arrived):
    return pl.pallas_call(
        line_kernel,
        out_shape=jax.ShapeDtypeStruct((16, 8, HALF), BF16),
        scratch_shapes=[pltpu.VMEM((8, SLAB_ROWS, LANES), F32)],
        compiler_params=params(),
        name="line_copies",
    )(arrived)


def restore_kernel(core_ref, own_ref, other_ref, out_ref):
    order = owner_order(True)
    mine = (pl.program_id(0) // CHUNKS) == core_ref[0]

    @pl.when(mine)
    def _():
        out_ref[...] = jnp.dot(order, own_ref[...], preferred_element_type=F32).astype(BF16)

    @pl.when(jnp.logical_not(mine))
    def _():
        out_ref[...] = jnp.dot(order, other_ref[...], preferred_element_type=F32).astype(BF16)


def restore(core, own, other):
    return pl.pallas_call(
        restore_kernel,
        out_shape=jax.ShapeDtypeStruct((ROWS, WIDTH), BF16),
        grid_spec=pltpu.PrefetchScalarGridSpec(
            num_scalar_prefetch=1,
            grid=(2 * CHUNKS,),
            in_specs=[
                pl.BlockSpec((ROWS, CHUNK), lambda i, core: (0, i % CHUNKS)),
                pl.BlockSpec((ROWS, CHUNK), lambda i, core: (0, i % CHUNKS)),
            ],
            out_specs=pl.BlockSpec((ROWS, CHUNK), lambda i, core: (0, i)),
        ),
        compiler_params=params(),
        name="restore",
    )(core, own, other)


def shards(grad_codes, scales, feedback, master, moment, second):
    core = lax.axis_index("core").astype(jnp.int32).reshape(1)
    codes, feed = grad_codes[0, 0], feedback[0, 0]
    turned = jnp.swapaxes(scales[0, 0], 0, 1)
    swap = [(0, 1), (1, 0)]
    given = compensate(1 - core, codes, turned, feed)
    taken = lax.ppermute(given, "core", swap)
    kept = compensate(core, codes, turned, feed)
    chip = pair_sum(kept, taken).reshape(16, 8, HALF)
    plane = plane_sum(lax.all_to_all(chip, ("x", "y"), 0, 0, tiled=True))
    line = lax.all_to_all(plane, ("zl", "zh"), 0, 0, tiled=True)
    slab = lambda a: a.reshape(SLAB_ROWS, LANES)
    adam_dir, new_master, copies = adam(line, slab(master), slab(moment), slab(second))
    owned = line_copies(lax.all_to_all(copies, ("zl", "zh"), 0, 0, tiled=True))
    mine = lax.all_to_all(owned, ("x", "y"), 0, 0, tiled=True).reshape(ROWS, HALF)
    theirs = lax.ppermute(mine, "core", swap)
    weights = restore(core, mine, theirs)
    return adam_dir.reshape(1, 1, HALF), new_master.reshape(1, 1, HALF), weights


def solution(mesh):
    fine = Mesh(mesh.devices.reshape(SIZES), AXES)
    wide, node = ("y", "zh", "core"), ("zl", "x")
    placed = (
        P(wide, node, None, None),
        P(wide, node, None, None),
        P(wide, node, None, None),
        P(node, wide, None),
        P(node, wide, None),
        P(node, wide, None),
    )
    return jax.shard_map(
        shards,
        mesh=fine,
        in_specs=placed,
        out_specs=(P(node, wide, None), P(node, wide, None), P()),
        check_vma=False,
    )
```

```python
import functools

import jax
import jax.numpy as jnp
from jax import lax
from jax.experimental import pallas as pl
from jax.experimental.pallas import tpu as pltpu
from jax.sharding import Mesh
from jax.sharding import PartitionSpec as P

beta_one = 0.9
beta_two = 0.999
adam_count = 100.0
adam_epsilon = 1e-08
learn_rate = 0.02

AXES = ("y", "zh", "core", "zl", "x")
SIZES = (4, 2, 2, 4, 4)
ROWS = 128
WIDTH = 9216
HALF = WIDTH // 2
LANES = 128
CHUNKS = 4
CHUNK = HALF // CHUNKS
PER_CHUNK = CHUNK // LANES
SLAB_ROWS = HALF // LANES
F32 = jnp.float32
BF16 = jnp.bfloat16
VMEM_LIMIT = 32 * 1024 * 1024
WHOLE = pl.BlockSpec(memory_space=pltpu.VMEM)
SCALAR = pl.BlockSpec(memory_space=pltpu.SMEM)
FAR = pl.BlockSpec(memory_space=pltpu.HBM)


def params():
    return pltpu.CompilerParams(vmem_limit_bytes=VMEM_LIMIT)


def in_hbm(array):
    return pltpu.with_memory_space_constraint(array, pltpu.HBM)


def shifted(stage, step):
    pairs = []
    for y in range(4):
        for zh in range(2):
            for core in range(2):
                for zl in range(4):
                    for x in range(4):
                        flat = lambda y, x: (((y * 2 + zh) * 2 + core) * 4 + zl) * 4 + x
                        along_x = core == stage
                        to = flat(y, (x + step) % 4) if along_x else flat((y + step) % 4, x)
                        pairs.append((flat(y, x), to))
    return pairs


SWAP = [(i, i ^ 16) for i in range(256)]


def send(array, stage, step):
    return lax.ppermute(array, AXES, shifted(stage, step))


def swap_cores(array):
    return lax.ppermute(array, AXES, SWAP)


def order(place, half, transposed):
    x0, y0 = place % 4, place // 64
    sent = lax.broadcasted_iota(jnp.int32, (ROWS, ROWS), 1 if transposed else 0)
    flat = lax.broadcasted_iota(jnp.int32, (ROWS, ROWS), 0 if transposed else 1)
    a0, a_step = jnp.where(half == 0, x0, y0), jnp.where(half == 0, 8, 2)
    b0, b_step = jnp.where(half == 0, y0, x0), jnp.where(half == 0, 2, 8)
    a, b = (sent // 32 + a0) % 4, (sent // 8 % 4 + b0) % 4
    return (sent // 2 % 4 * 32 + a * a_step + b * b_step + sent % 2 == flat).astype(F32).astype(BF16)


def compensate_kernel(other, place_ref, codes_hbm, scales_hbm, feedback_hbm, out_ref, codes, scales, feedback, turned, sems):
    core = place_ref[0] // 16 % 2
    half = 1 - core if other else core
    copies = [pltpu.make_async_copy(scales_hbm, scales, sems.at[2 * CHUNKS])]
    for i in range(CHUNKS):
        columns = pl.ds(pl.multiple_of(half * HALF + i * CHUNK, LANES), CHUNK)
        copies.append(pltpu.make_async_copy(codes_hbm.at[:, columns], codes.at[i], sems.at[2 * i]))
        copies.append(pltpu.make_async_copy(feedback_hbm.at[:, columns], feedback.at[i], sems.at[2 * i + 1]))
    for copy in copies:
        copy.start()
    moved = order(place_ref[0], half, False)
    copies[0].wait()
    turned[0:SLAB_ROWS, :] = scales[pl.ds(half * SLAB_ROWS, SLAB_ROWS), :]
    scale = turned[...].T
    for i in range(CHUNKS):
        copies[1 + 2 * i].wait()
        copies[2 + 2 * i].wait()
        for block in range(PER_CHUNK):
            columns = slice(block * LANES, (block + 1) * LANES)
            at = i * PER_CHUNK + block
            dequant = codes[i, :, columns].astype(F32) * scale[:, at : at + 1]
            compensated = (dequant + feedback[i, :, columns].astype(F32)).astype(BF16)
            out_ref[:, at * LANES : (at + 1) * LANES] = jnp.dot(moved, compensated, preferred_element_type=F32).astype(BF16)


def compensate(other, place, codes, scales, feedback):
    return pl.pallas_call(
        functools.partial(compensate_kernel, other),
        out_shape=jax.ShapeDtypeStruct((ROWS, HALF), BF16),
        in_specs=[SCALAR, FAR, FAR, FAR],
        out_specs=WHOLE,
        scratch_shapes=[
            pltpu.VMEM((CHUNKS, ROWS, CHUNK), jnp.int32),
            pltpu.VMEM((WIDTH // LANES, ROWS), F32),
            pltpu.VMEM((CHUNKS, ROWS, CHUNK), BF16),
            pltpu.VMEM((ROWS, LANES), F32),
            pltpu.SemaphoreType.DMA((2 * CHUNKS + 1,)),
        ],
        compiler_params=params(),
        cost_estimate=pl.CostEstimate(flops=2 * ROWS * ROWS * HALF, bytes_accessed=8 * ROWS * HALF, transcendentals=0),
        name="compensate",
    )(place, in_hbm(codes), in_hbm(scales), in_hbm(feedback))


def pair_sum_kernel(own_ref, other_ref, *out_refs):
    for piece, out_ref in enumerate(out_refs):
        rows = slice(piece * 32, (piece + 1) * 32)
        out_ref[...] = (own_ref[rows, :].astype(F32) + other_ref[rows, :].astype(F32)).astype(BF16)


def pair_sum(own, other):
    return pl.pallas_call(
        pair_sum_kernel,
        out_shape=[jax.ShapeDtypeStruct((32, HALF), BF16)] * 4,
        in_specs=[WHOLE] * 2,
        out_specs=[WHOLE] * 4,
        compiler_params=params(),
        name="pair_sum",
    )(own, other)


def total_of(refs, rows):
    first, *others = [ref[rows, :].astype(F32) for ref in refs]
    return functools.reduce(lambda a, b: a + b, others, first)


def first_sum_kernel(a_ref, b_ref, c_ref, d_ref, *out_refs):
    for piece, out_ref in enumerate(out_refs):
        out_ref[...] = total_of((a_ref, b_ref, c_ref, d_ref), slice(piece * 8, (piece + 1) * 8)).astype(BF16)


def first_sum(parts):
    return pl.pallas_call(
        first_sum_kernel,
        out_shape=[jax.ShapeDtypeStruct((8, HALF), BF16)] * 4,
        in_specs=[WHOLE] * 4,
        out_specs=[WHOLE] * 4,
        compiler_params=params(),
        name="first_sum",
    )(*parts)


def second_sum_kernel(a_ref, b_ref, c_ref, d_ref, out_ref, spread):
    total = total_of((a_ref, b_ref, c_ref, d_ref), slice(None))
    for block in range(SLAB_ROWS):
        spread[:, block, :] = total[:, block * LANES : (block + 1) * LANES]
    out_ref[...] = spread[...].astype(BF16)


def second_sum(parts):
    return pl.pallas_call(
        second_sum_kernel,
        out_shape=jax.ShapeDtypeStruct((8, SLAB_ROWS, LANES), BF16),
        in_specs=[WHOLE] * 4,
        out_specs=WHOLE,
        scratch_shapes=[pltpu.VMEM((8, SLAB_ROWS, LANES), F32)],
        compiler_params=params(),
        name="second_sum",
    )(*parts)


def adam_kernel(arrived_ref, master_ref, moment_ref, second_ref, dir_ref, new_ref, copies_ref):
    grad = jnp.sum(arrived_ref[...].astype(F32), axis=0) / 256.0
    first = beta_one * moment_ref[...] + (1.0 - beta_one) * grad
    squared = beta_two * second_ref[...] + (1.0 - beta_two) * grad * grad
    first_hat = first / (1.0 - beta_one**adam_count)
    squared_hat = squared / (1.0 - beta_two**adam_count)
    adam_dir = first_hat / (jnp.sqrt(squared_hat) + adam_epsilon)
    new_master = master_ref[...] - learn_rate * adam_dir
    dir_ref[...] = adam_dir
    new_ref[...] = new_master
    copies_ref[...] = jnp.broadcast_to(new_master.astype(BF16)[None], copies_ref.shape)


def adam(arrived, master, moment, second):
    slab = jax.ShapeDtypeStruct((SLAB_ROWS, LANES), F32)
    return pl.pallas_call(
        adam_kernel,
        out_shape=(slab, slab, jax.ShapeDtypeStruct((8, SLAB_ROWS, LANES), BF16)),
        in_specs=[WHOLE] * 4,
        out_specs=[WHOLE] * 3,
        compiler_params=params(),
        name="adam",
    )(arrived, master, moment, second)


def line_kernel(in_ref, out_ref, spread):
    spread[...] = in_ref[...].astype(F32)
    for block in range(SLAB_ROWS):
        out_ref[:, block * LANES : (block + 1) * LANES] = spread[:, block, :].astype(BF16)


def line_rows(arrived):
    return pl.pallas_call(
        line_kernel,
        out_shape=jax.ShapeDtypeStruct((8, HALF), BF16),
        in_specs=[WHOLE],
        out_specs=WHOLE,
        scratch_shapes=[pltpu.VMEM((8, SLAB_ROWS, LANES), F32)],
        compiler_params=params(),
        name="line_rows",
    )(arrived)


def join_kernel(a_ref, b_ref, c_ref, d_ref, out_ref):
    for piece, ref in enumerate((a_ref, b_ref, c_ref, d_ref)):
        out_ref[piece * 8 : (piece + 1) * 8, :] = ref[...]


def join(parts):
    return pl.pallas_call(
        join_kernel,
        out_shape=jax.ShapeDtypeStruct((32, HALF), BF16),
        in_specs=[WHOLE] * 4,
        out_specs=WHOLE,
        compiler_params=params(),
        name="join",
    )(*parts)


def restore_kernel(other, place_ref, a_ref, b_ref, c_ref, d_ref, *refs):
    out_hbm, staged, sems = refs[-3:]
    core = place_ref[0] // 16 % 2
    half = 1 - core if other else core
    moved = order(place_ref[0], half, True)
    copies = []
    for i in range(CHUNKS):
        columns = slice(i * CHUNK, (i + 1) * CHUNK)
        rows = jnp.concatenate([ref[:, columns] for ref in (a_ref, b_ref, c_ref, d_ref)], axis=0)
        staged[i] = jnp.dot(moved, rows, preferred_element_type=F32).astype(BF16)
        to = pl.ds(pl.multiple_of(half * HALF + i * CHUNK, LANES), CHUNK)
        copies.append(pltpu.make_async_copy(staged.at[i], out_hbm.at[:, to], sems.at[i]))
        copies[-1].start()
    for copy in copies:
        copy.wait()


def restore(other, place, parts, held=()):
    return pl.pallas_call(
        functools.partial(restore_kernel, other),
        out_shape=jax.ShapeDtypeStruct((ROWS, WIDTH), BF16),
        in_specs=[SCALAR] + [WHOLE] * 4 + [FAR] * len(held),
        out_specs=FAR,
        scratch_shapes=[pltpu.VMEM((CHUNKS, ROWS, CHUNK), BF16), pltpu.SemaphoreType.DMA((CHUNKS,))],
        input_output_aliases={5: 0} if held else {},
        compiler_params=params(),
        name="restore",
    )(place, *parts, *held)


def shards(grad_codes, scales, feedback, master, moment, second):
    place = lax.axis_index(AXES).astype(jnp.int32).reshape(1)
    codes, feed = grad_codes[0, 0], feedback[0, 0]
    turned = jnp.swapaxes(scales[0, 0], 0, 1)
    given = compensate(True, place, codes, turned, feed)
    taken = swap_cores(given)
    kept = compensate(False, place, codes, turned, feed)
    first = pair_sum(kept, taken)
    second_parts = first_sum([first[0]] + [send(first[step], 0, step) for step in (1, 2, 3)])
    plane = second_sum([second_parts[0]] + [send(second_parts[step], 1, step) for step in (1, 2, 3)])
    line = lax.all_to_all(plane, ("zl", "zh"), 0, 0, tiled=True)
    slab = lambda a: a.reshape(SLAB_ROWS, LANES)
    adam_dir, new_master, copies = adam(line, slab(master), slab(moment), slab(second))
    owned = line_rows(lax.all_to_all(copies, ("zl", "zh"), 0, 0, tiled=True))
    joined = join([owned] + [send(owned, 1, 4 - place_of) for place_of in (1, 2, 3)])
    mine = [joined] + [send(joined, 0, 4 - place_of) for place_of in (1, 2, 3)]
    theirs = [swap_cores(part) for part in mine]
    half = restore(False, place, mine)
    weights = restore(True, place, theirs, (half,))
    return adam_dir.reshape(1, 1, HALF), new_master.reshape(1, 1, HALF), weights


def solution(mesh):
    fine = Mesh(mesh.devices.reshape(SIZES), AXES)
    wide, node = ("y", "zh", "core"), ("zl", "x")
    placed = (
        P(wide, node, None, None),
        P(wide, node, None, None),
        P(wide, node, None, None),
        P(node, wide, None),
        P(node, wide, None),
        P(node, wide, None),
    )
    return jax.shard_map(
        shards,
        mesh=fine,
        in_specs=placed,
        out_specs=(P(node, wide, None), P(node, wide, None), P()),
        check_vma=False,
    )
```

```python
import functools

import jax
import jax.numpy as jnp
from jax import lax
from jax.experimental import pallas as pl
from jax.experimental.pallas import tpu as pltpu
from jax.sharding import Mesh
from jax.sharding import PartitionSpec as P

beta_one = 0.9
beta_two = 0.999
adam_count = 100.0
adam_epsilon = 1e-08
learn_rate = 0.02

AXES = ("y", "zh", "core", "zl", "x")
SIZES = (4, 2, 2, 4, 4)
ROWS = 128
WIDTH = 9216
HALF = WIDTH // 2
LANES = 128
CHUNKS = 6
CHUNK = HALF // CHUNKS
PER_CHUNK = CHUNK // LANES
SLAB_ROWS = HALF // LANES
F32 = jnp.float32
BF16 = jnp.bfloat16
VMEM_LIMIT = 32 * 1024 * 1024
WHOLE = pl.BlockSpec(memory_space=pltpu.VMEM)
SCALAR = pl.BlockSpec(memory_space=pltpu.SMEM)
FAR = pl.BlockSpec(memory_space=pltpu.HBM)


def params():
    return pltpu.CompilerParams(vmem_limit_bytes=VMEM_LIMIT)


def in_hbm(array):
    return pltpu.with_memory_space_constraint(array, pltpu.HBM)


def shifted(step):
    flat = lambda y, zh, core, zl, x: (((y * 2 + zh) * 2 + core) * 4 + zl) * 4 + x
    pairs = []
    for i in range(256):
        x, zl, core, zh, y = i % 4, i // 4 % 4, i // 16 % 2, i // 32 % 2, i // 64
        to = flat((y + step) % 4, zh, core, zl, x) if core else flat(y, zh, core, zl, (x + step) % 4)
        pairs.append((i, to))
    return pairs


SWAP = [(i, i ^ 16) for i in range(256)]


def send(array, step):
    return lax.ppermute(array, AXES, shifted(step))


def swap_cores(array):
    return lax.ppermute(array, AXES, SWAP)


def owner_groups():
    flat = lambda y, zh, core, zl, x: (((y * 2 + zh) * 2 + core) * 4 + zl) * 4 + x
    groups = [[flat(y, zh, 0, zl, x) for y in range(4) for zl in range(4) for zh in range(2)] for x in range(4)]
    return groups + [[flat(y, zh, 1, zl, x) for x in range(4) for zl in range(4) for zh in range(2)] for y in range(4)]


def exchange(array):
    return lax.all_to_all(array, AXES, 0, 0, axis_index_groups=owner_groups(), tiled=True)


def order(place, half, transposed):
    x0, y0 = place % 4, place // 64
    sent = lax.broadcasted_iota(jnp.int32, (ROWS, ROWS), 1 if transposed else 0)
    flat = lax.broadcasted_iota(jnp.int32, (ROWS, ROWS), 0 if transposed else 1)
    a0, a_step = jnp.where(half == 0, x0, y0), jnp.where(half == 0, 8, 2)
    a, b = (sent // 32 + a0) % 4, sent // 8 % 4
    return (sent // 2 % 4 * 32 + a * a_step + b * (10 - a_step) + sent % 2 == flat).astype(F32).astype(BF16)


def compensate_kernel(other, place_ref, codes_hbm, scales_hbm, feedback_hbm, out_ref, codes, scales, feedback, turned, summed, sems):
    core = place_ref[0] // 16 % 2
    half = 1 - core if other else core
    copies = [pltpu.make_async_copy(scales_hbm, scales, sems.at[2 * CHUNKS])]
    for i in range(CHUNKS):
        columns = pl.ds(pl.multiple_of(half * HALF + i * CHUNK, LANES), CHUNK)
        copies.append(pltpu.make_async_copy(codes_hbm.at[:, columns], codes.at[i], sems.at[2 * i]))
        copies.append(pltpu.make_async_copy(feedback_hbm.at[:, columns], feedback.at[i], sems.at[2 * i + 1]))
    for copy in copies:
        copy.start()
    moved = order(place_ref[0], half, False)
    copies[0].wait()
    turned[0:SLAB_ROWS, :] = scales[pl.ds(half * SLAB_ROWS, SLAB_ROWS), :]
    scale = turned[...].T
    for i in range(CHUNKS):
        copies[1 + 2 * i].wait()
        copies[2 + 2 * i].wait()
        for block in range(PER_CHUNK):
            columns = slice(block * LANES, (block + 1) * LANES)
            at = i * PER_CHUNK + block
            dequant = codes[i, :, columns].astype(F32) * scale[:, at : at + 1]
            summed[:, columns] = (dequant + feedback[i, :, columns].astype(F32)).astype(BF16)
        out_ref[:, i * CHUNK : (i + 1) * CHUNK] = jnp.dot(moved, summed[...], preferred_element_type=F32).astype(BF16)


def compensate(other, place, codes, scales, feedback):
    return pl.pallas_call(
        functools.partial(compensate_kernel, other),
        out_shape=jax.ShapeDtypeStruct((ROWS, HALF), BF16),
        in_specs=[SCALAR, FAR, FAR, FAR],
        out_specs=WHOLE,
        scratch_shapes=[
            pltpu.VMEM((CHUNKS, ROWS, CHUNK), jnp.int32),
            pltpu.VMEM((WIDTH // LANES, ROWS), F32),
            pltpu.VMEM((CHUNKS, ROWS, CHUNK), BF16),
            pltpu.VMEM((ROWS, LANES), F32),
            pltpu.VMEM((ROWS, CHUNK), BF16),
            pltpu.SemaphoreType.DMA((2 * CHUNKS + 1,)),
        ],
        compiler_params=params(),
        cost_estimate=pl.CostEstimate(flops=2 * ROWS * ROWS * HALF, bytes_accessed=8 * ROWS * HALF, transcendentals=0),
        name="compensate",
    )(place, in_hbm(codes), in_hbm(scales), in_hbm(feedback))


def pair_sum_kernel(own_ref, other_ref, *out_refs):
    for piece, out_ref in enumerate(out_refs):
        rows = slice(piece * 32, (piece + 1) * 32)
        out_ref[...] = (own_ref[rows, :].astype(F32) + other_ref[rows, :].astype(F32)).astype(BF16)


def pair_sum(own, other):
    return pl.pallas_call(
        pair_sum_kernel,
        out_shape=[jax.ShapeDtypeStruct((32, HALF), BF16)] * 4,
        in_specs=[WHOLE] * 2,
        out_specs=[WHOLE] * 4,
        compiler_params=params(),
        name="pair_sum",
    )(own, other)


def total_of(refs, rows):
    first, *others = [ref[rows, :].astype(F32) for ref in refs]
    return functools.reduce(lambda a, b: a + b, others, first)


def first_sum_kernel(a_ref, b_ref, c_ref, d_ref, out_ref, columns):
    total = total_of((a_ref, b_ref, c_ref, d_ref), slice(None))
    for block in range(SLAB_ROWS):
        columns[block * 32 : (block + 1) * 32, :] = total[:, block * LANES : (block + 1) * LANES]
    for row in range(32):
        out_ref[row] = columns[pl.ds(row, SLAB_ROWS, stride=32), :].astype(BF16)


def first_sum(parts):
    return pl.pallas_call(
        first_sum_kernel,
        out_shape=jax.ShapeDtypeStruct((32, SLAB_ROWS, LANES), BF16),
        in_specs=[WHOLE] * 4,
        out_specs=WHOLE,
        scratch_shapes=[pltpu.VMEM((SLAB_ROWS * 32, LANES), F32)],
        compiler_params=params(),
        name="first_sum",
    )(*parts)


def adam_kernel(arrived_ref, master_ref, moment_ref, second_ref, dir_ref, new_ref, copies_ref):
    grad = jnp.sum(arrived_ref[...].astype(F32), axis=0) / 256.0
    first = beta_one * moment_ref[...] + (1.0 - beta_one) * grad
    squared = beta_two * second_ref[...] + (1.0 - beta_two) * grad * grad
    first_hat = first / (1.0 - beta_one**adam_count)
    squared_hat = squared / (1.0 - beta_two**adam_count)
    adam_dir = first_hat / (jnp.sqrt(squared_hat) + adam_epsilon)
    new_master = master_ref[...] - learn_rate * adam_dir
    dir_ref[...] = adam_dir
    new_ref[...] = new_master
    copies_ref[...] = jnp.broadcast_to(new_master.astype(BF16)[None], copies_ref.shape)


def adam(arrived, master, moment, second):
    slab = jax.ShapeDtypeStruct((SLAB_ROWS, LANES), F32)
    return pl.pallas_call(
        adam_kernel,
        out_shape=(slab, slab, jax.ShapeDtypeStruct((32, SLAB_ROWS, LANES), BF16)),
        in_specs=[WHOLE] * 4,
        out_specs=[WHOLE] * 3,
        compiler_params=params(),
        name="adam",
    )(arrived, master, moment, second)


def line_kernel(in_ref, out_ref, spread):
    spread[...] = in_ref[...].astype(F32)
    for block in range(SLAB_ROWS):
        out_ref[:, block * LANES : (block + 1) * LANES] = spread[:, block, :].astype(BF16)


def line_rows(arrived):
    return pl.pallas_call(
        line_kernel,
        out_shape=jax.ShapeDtypeStruct((32, HALF), BF16),
        in_specs=[WHOLE],
        out_specs=WHOLE,
        scratch_shapes=[pltpu.VMEM((32, SLAB_ROWS, LANES), F32)],
        compiler_params=params(),
        name="line_rows",
    )(arrived)


def restore_kernel(other, place_ref, a_ref, b_ref, c_ref, d_ref, *refs):
    out_hbm, staged, sems = refs[-3:]
    core = place_ref[0] // 16 % 2
    half = 1 - core if other else core
    moved = order(place_ref[0], half, True)
    copies = []
    for i in range(CHUNKS):
        columns = slice(i * CHUNK, (i + 1) * CHUNK)
        rows = jnp.concatenate([ref[:, columns] for ref in (a_ref, b_ref, c_ref, d_ref)], axis=0)
        staged[i] = jnp.dot(moved, rows, preferred_element_type=F32).astype(BF16)
        to = pl.ds(pl.multiple_of(half * HALF + i * CHUNK, LANES), CHUNK)
        copies.append(pltpu.make_async_copy(staged.at[i], out_hbm.at[:, to], sems.at[i]))
        copies[-1].start()
    for copy in copies:
        copy.wait()


def restore(other, place, parts, held=()):
    return pl.pallas_call(
        functools.partial(restore_kernel, other),
        out_shape=jax.ShapeDtypeStruct((ROWS, WIDTH), BF16),
        in_specs=[SCALAR] + [WHOLE] * 4 + [FAR] * len(held),
        out_specs=FAR,
        scratch_shapes=[pltpu.VMEM((CHUNKS, ROWS, CHUNK), BF16), pltpu.SemaphoreType.DMA((CHUNKS,))],
        input_output_aliases={5: 0} if held else {},
        compiler_params=params(),
        name="restore",
    )(place, *parts, *held)


def shards(grad_codes, scales, feedback, master, moment, second):
    place = lax.axis_index(AXES).astype(jnp.int32).reshape(1)
    codes, feed = grad_codes[0, 0], feedback[0, 0]
    turned = jnp.swapaxes(scales[0, 0], 0, 1)
    given = compensate(True, place, codes, turned, feed)
    taken = swap_cores(given)
    kept = compensate(False, place, codes, turned, feed)
    first = pair_sum(kept, taken)
    plane = first_sum([first[0]] + [send(first[step], step) for step in (1, 2, 3)])
    slab = lambda a: a.reshape(SLAB_ROWS, LANES)
    adam_dir, new_master, copies = adam(exchange(plane), slab(master), slab(moment), slab(second))
    joined = line_rows(exchange(copies))
    mine = [joined] + [send(joined, 4 - place_of) for place_of in (1, 2, 3)]
    adam_dir, new_master = adam_dir.reshape(1, 1, HALF), new_master.reshape(1, 1, HALF)
    mine[2], adam_dir, new_master = lax.optimization_barrier((mine[2], adam_dir, new_master))
    theirs = [swap_cores(part) for part in mine]
    half = restore(False, place, mine)
    weights = restore(True, place, theirs, (half,))
    return adam_dir, new_master, weights


def solution(mesh):
    fine = Mesh(mesh.devices.reshape(SIZES), AXES)
    wide, node = ("y", "zh", "core"), ("zl", "x")
    placed = (
        P(wide, node, None, None),
        P(wide, node, None, None),
        P(wide, node, None, None),
        P(node, wide, None),
        P(node, wide, None),
        P(node, wide, None),
    )
    return jax.shard_map(
        shards,
        mesh=fine,
        in_specs=placed,
        out_specs=(P(node, wide, None), P(node, wide, None), P()),
        check_vma=False,
    )
```

```python
import functools

import jax
import jax.numpy as jnp
from jax import lax
from jax.experimental import pallas as pl
from jax.experimental.pallas import tpu as pltpu
from jax.sharding import Mesh
from jax.sharding import PartitionSpec as P

beta_one = 0.9
beta_two = 0.999
adam_count = 100.0
adam_epsilon = 1e-08
learn_rate = 0.02

AXES = ("y", "zh", "core", "zl", "x")
SIZES = (4, 2, 2, 4, 4)
ROWS = 128
WIDTH = 9216
HALF = WIDTH // 2
LANES = 128
CHUNKS = 3
CHUNK = HALF // CHUNKS
PER_CHUNK = CHUNK // LANES
SLAB_ROWS = HALF // LANES
SLAB = (2, HALF // 2)
F32 = jnp.float32
BF16 = jnp.bfloat16
VMEM_LIMIT = 32 * 1024 * 1024
WHOLE = pl.BlockSpec(memory_space=pltpu.VMEM)
SCALAR = pl.BlockSpec(memory_space=pltpu.SMEM)
FAR = pl.BlockSpec(memory_space=pltpu.HBM)


def params():
    return pltpu.CompilerParams(vmem_limit_bytes=VMEM_LIMIT)


def in_hbm(array):
    return pltpu.with_memory_space_constraint(array, pltpu.HBM)


def device(x, y, z, core):
    return (((y * 2 + z // 4) * 2 + core) * 4 + z % 4) * 4 + x


def paired(core, pair, which):
    return (2 * pair + core + which) % 8


def large_groups():
    groups = [[device(x, y, paired(0, p, k), 0) for x in range(4) for k in range(2)] for y in range(4) for p in range(4)]
    return groups + [[device(x, y, paired(1, p, k), 1) for y in range(4) for k in range(2)] for x in range(4) for p in range(4)]


def small_groups():
    groups = [[device(x, y, paired(0, p, k), 0) for y in range(4) for p in range(4)] for x in range(4) for k in range(2)]
    return groups + [[device(x, y, paired(1, p, k), 1) for x in range(4) for p in range(4)] for y in range(4) for k in range(2)]


SWAP = [(i, i ^ 16) for i in range(256)]


def swap_cores(array):
    return lax.ppermute(array, AXES, SWAP)


def exchange(array, groups):
    return lax.all_to_all(array, AXES, 0, 0, axis_index_groups=groups, tiled=True)


def order(half, transposed):
    sent = lax.broadcasted_iota(jnp.int32, (ROWS, ROWS), 1 if transposed else 0)
    flat = lax.broadcasted_iota(jnp.int32, (ROWS, ROWS), 0 if transposed else 1)
    a, k, b, p = sent // 32, sent // 16 % 2, sent // 4 % 4, sent % 4
    z = (2 * p + k + half) % 8
    a_step = jnp.where(half == 0, 8, 2)
    return (z % 4 * 32 + a * a_step + b * (10 - a_step) + z // 4 == flat).astype(F32).astype(BF16)


def compensate_kernel(other, core_ref, codes_hbm, scales_hbm, feedback_hbm, out_ref, codes, scales, feedback, turned, summed, sems):
    core = core_ref[0]
    half = 1 - core if other else core
    copies = [pltpu.make_async_copy(scales_hbm, scales, sems.at[2 * CHUNKS])]
    for i in range(CHUNKS):
        columns = pl.ds(pl.multiple_of(half * HALF + i * CHUNK, LANES), CHUNK)
        copies.append(pltpu.make_async_copy(codes_hbm.at[:, columns], codes.at[i], sems.at[2 * i]))
        copies.append(pltpu.make_async_copy(feedback_hbm.at[:, columns], feedback.at[i], sems.at[2 * i + 1]))
    for copy in copies:
        copy.start()
    moved = order(half, False)
    copies[0].wait()
    turned[0:SLAB_ROWS, :] = scales[pl.ds(half * SLAB_ROWS, SLAB_ROWS), :]
    scale = turned[...].T
    for i in range(CHUNKS):
        copies[1 + 2 * i].wait()
        copies[2 + 2 * i].wait()
        for block in range(PER_CHUNK):
            columns = slice(block * LANES, (block + 1) * LANES)
            at = i * PER_CHUNK + block
            dequant = codes[i, :, columns].astype(F32) * scale[:, at : at + 1]
            summed[i, :, columns] = (dequant + feedback[i, :, columns].astype(F32)).astype(BF16)
    for i in range(CHUNKS):
        out_ref[:, i * CHUNK : (i + 1) * CHUNK] = jnp.dot(moved, summed[i], preferred_element_type=F32).astype(BF16)


def compensate(other, core, codes, scales, feedback):
    return pl.pallas_call(
        functools.partial(compensate_kernel, other),
        out_shape=jax.ShapeDtypeStruct((ROWS, HALF), BF16),
        in_specs=[SCALAR, FAR, FAR, FAR],
        out_specs=WHOLE,
        scratch_shapes=[
            pltpu.VMEM((CHUNKS, ROWS, CHUNK), jnp.int32),
            pltpu.VMEM((WIDTH // LANES, ROWS), F32),
            pltpu.VMEM((CHUNKS, ROWS, CHUNK), BF16),
            pltpu.VMEM((ROWS, LANES), F32),
            pltpu.VMEM((CHUNKS, ROWS, CHUNK), BF16),
            pltpu.SemaphoreType.DMA((2 * CHUNKS + 1,)),
        ],
        compiler_params=params(),
        cost_estimate=pl.CostEstimate(flops=2 * ROWS * ROWS * HALF, bytes_accessed=8 * ROWS * HALF, transcendentals=0),
        name="compensate",
    )(core, in_hbm(codes), in_hbm(scales), in_hbm(feedback))


def pair_sum_kernel(own_ref, other_ref, out_ref):
    for piece in range(8):
        rows = slice(piece * 16, (piece + 1) * 16)
        out_ref[piece] = (own_ref[rows, :].astype(F32) + other_ref[rows, :].astype(F32)).astype(BF16)


def pair_sum(own, other):
    return pl.pallas_call(
        pair_sum_kernel,
        out_shape=jax.ShapeDtypeStruct((8, 16, HALF), BF16),
        in_specs=[WHOLE] * 2,
        out_specs=WHOLE,
        compiler_params=params(),
        name="pair_sum",
    )(own, other)


def group_sum_kernel(in_ref, out_ref):
    for block in range(SLAB_ROWS):
        columns = slice(block * LANES, (block + 1) * LANES)
        out_ref[:, columns] = jnp.sum(in_ref[:, :, columns].astype(F32), axis=0).astype(BF16)


def group_sum(arrived):
    return pl.pallas_call(
        group_sum_kernel,
        out_shape=jax.ShapeDtypeStruct((16, HALF), BF16),
        in_specs=[WHOLE],
        out_specs=WHOLE,
        compiler_params=params(),
        name="group_sum",
    )(arrived)


def adam_kernel(arrived_ref, master_ref, moment_ref, second_ref, dir_ref, new_ref, copies_ref):
    total = jnp.sum(arrived_ref[...].astype(F32), axis=0)
    grad = jnp.concatenate([total[0:1], total[1:2]], axis=1) / 256.0
    first = beta_one * moment_ref[...] + (1.0 - beta_one) * grad
    squared = beta_two * second_ref[...] + (1.0 - beta_two) * grad * grad
    first_hat = first / (1.0 - beta_one**adam_count)
    squared_hat = squared / (1.0 - beta_two**adam_count)
    adam_dir = first_hat / (jnp.sqrt(squared_hat) + adam_epsilon)
    new_master = master_ref[...] - learn_rate * adam_dir
    dir_ref[...] = adam_dir
    new_ref[...] = new_master
    rows = jnp.concatenate([new_master[:, : SLAB[1]], new_master[:, SLAB[1] :]], axis=0)
    copies_ref[...] = jnp.broadcast_to(rows.astype(BF16)[None], copies_ref.shape)


def adam(arrived, master, moment, second):
    slab = jax.ShapeDtypeStruct((1, HALF), F32)
    return pl.pallas_call(
        adam_kernel,
        out_shape=(slab, slab, jax.ShapeDtypeStruct((16, *SLAB), BF16)),
        in_specs=[WHOLE] * 4,
        out_specs=[WHOLE] * 3,
        compiler_params=params(),
        name="adam",
    )(arrived, master, moment, second)


def copies_kernel(in_ref, out_ref):
    out_ref[...] = jnp.broadcast_to(in_ref[...][None], out_ref.shape)


def copies_of(rows):
    return pl.pallas_call(
        copies_kernel,
        out_shape=jax.ShapeDtypeStruct((8, 16, HALF), BF16),
        in_specs=[WHOLE],
        out_specs=WHOLE,
        compiler_params=params(),
        name="copies_of",
    )(rows)


def place_half(half, rows_ref, weights_hbm, staged, sems):
    moved = order(half, True)
    copies = []
    for i in range(CHUNKS):
        rows = rows_ref[:, i * CHUNK : (i + 1) * CHUNK]
        staged[i] = jnp.dot(moved, rows, preferred_element_type=F32).astype(BF16)
        to = pl.ds(pl.multiple_of(half * HALF + i * CHUNK, LANES), CHUNK)
        copies.append(pltpu.make_async_copy(staged.at[i], weights_hbm.at[:, to], sems.at[i]))
        copies[-1].start()
    return copies


def restore_own_kernel(core_ref, rows_ref, dir_ref, new_ref, weights_hbm, dir_hbm, new_hbm, staged, sems):
    copies = [
        pltpu.make_async_copy(dir_ref, dir_hbm, sems.at[CHUNKS]),
        pltpu.make_async_copy(new_ref, new_hbm, sems.at[CHUNKS + 1]),
    ]
    for copy in copies:
        copy.start()
    for copy in copies + place_half(core_ref[0], rows_ref, weights_hbm, staged, sems):
        copy.wait()


def restore_own(core, rows, adam_dir, new_master):
    slab = jax.ShapeDtypeStruct((1, HALF), F32)
    return pl.pallas_call(
        restore_own_kernel,
        out_shape=(jax.ShapeDtypeStruct((ROWS, WIDTH), BF16), slab, slab),
        in_specs=[SCALAR] + [WHOLE] * 3,
        out_specs=[FAR] * 3,
        scratch_shapes=[pltpu.VMEM((CHUNKS, ROWS, CHUNK), BF16), pltpu.SemaphoreType.DMA((CHUNKS + 2,))],
        compiler_params=params(),
        name="restore_own",
    )(core, rows, adam_dir, new_master)


def restore_other_kernel(core_ref, rows_ref, held_hbm, weights_hbm, staged, sems):
    for copy in place_half(1 - core_ref[0], rows_ref, weights_hbm, staged, sems):
        copy.wait()


def restore_other(core, rows, weights):
    return pl.pallas_call(
        restore_other_kernel,
        out_shape=jax.ShapeDtypeStruct((ROWS, WIDTH), BF16),
        in_specs=[SCALAR, WHOLE, FAR],
        out_specs=FAR,
        scratch_shapes=[pltpu.VMEM((CHUNKS, ROWS, CHUNK), BF16), pltpu.SemaphoreType.DMA((CHUNKS,))],
        input_output_aliases={2: 0},
        compiler_params=params(),
        name="restore_other",
    )(core, rows, weights)


def shards(grad_codes, scales, feedback, master, moment, second):
    core = lax.axis_index("core").astype(jnp.int32).reshape(1)
    codes, feed = grad_codes[0, 0], feedback[0, 0]
    turned = jnp.swapaxes(scales[0, 0], 0, 1)
    given = compensate(True, core, codes, turned, feed)
    taken = swap_cores(given)
    kept = compensate(False, core, codes, turned, feed)
    partial = group_sum(exchange(pair_sum(kept, taken), large_groups()))
    arrived = exchange(partial.reshape(16, *SLAB), small_groups())
    adam_dir, new_master, copies = adam(arrived, master[0], moment[0], second[0])
    rows = exchange(copies, small_groups()).reshape(16, HALF)
    mine = exchange(copies_of(rows), large_groups()).reshape(ROWS, HALF)
    theirs = swap_cores(mine)
    weights, adam_dir, new_master = restore_own(core, mine, adam_dir, new_master)
    weights = restore_other(core, theirs, weights)
    return adam_dir[None], new_master[None], weights


def solution(mesh):
    fine = Mesh(mesh.devices.reshape(SIZES), AXES)
    wide, node = ("y", "zh", "core"), ("zl", "x")
    placed = (
        P(wide, node, None, None),
        P(wide, node, None, None),
        P(wide, node, None, None),
        P(node, wide, None),
        P(node, wide, None),
        P(node, wide, None),
    )
    return jax.shard_map(
        shards,
        mesh=fine,
        in_specs=placed,
        out_specs=(P(node, wide, None), P(node, wide, None), P()),
        check_vma=False,
    )
```

```python
import functools

import jax
import jax.numpy as jnp
from jax import lax
from jax.experimental import pallas as pl
from jax.experimental.pallas import tpu as pltpu
from jax.sharding import Mesh
from jax.sharding import PartitionSpec as P

beta_one = 0.9
beta_two = 0.999
adam_count = 100.0
adam_epsilon = 1e-08
learn_rate = 0.02

AXES = ("y", "zh", "core", "zl", "x")
SIZES = (4, 2, 2, 4, 4)
ROWS = 128
WIDTH = 9216
HALF = WIDTH // 2
LANES = 128
CHUNKS = 3
CHUNK = HALF // CHUNKS
PER_CHUNK = CHUNK // LANES
SLAB_ROWS = HALF // LANES
SLAB = (2, HALF // 2)
F32 = jnp.float32
BF16 = jnp.bfloat16
VMEM_LIMIT = 32 * 1024 * 1024
WHOLE = pl.BlockSpec(memory_space=pltpu.VMEM)
SCALAR = pl.BlockSpec(memory_space=pltpu.SMEM)
FAR = pl.BlockSpec(memory_space=pltpu.HBM)


def params():
    return pltpu.CompilerParams(vmem_limit_bytes=VMEM_LIMIT)


def in_hbm(array):
    return pltpu.with_memory_space_constraint(array, pltpu.HBM)


def device(x, y, z, core):
    return (((y * 2 + z // 4) * 2 + core) * 4 + z % 4) * 4 + x


def paired(core, pair, which):
    return (2 * pair + core + which) % 8


def large_groups():
    groups = [[device(x, y, paired(0, p, k), 0) for x in range(4) for k in range(2)] for y in range(4) for p in range(4)]
    return groups + [[device(x, y, paired(1, p, k), 1) for y in range(4) for k in range(2)] for x in range(4) for p in range(4)]


def small_groups():
    groups = [[device(x, y, paired(0, p, k), 0) for y in range(4) for p in range(4)] for x in range(4) for k in range(2)]
    return groups + [[device(x, y, paired(1, p, k), 1) for x in range(4) for p in range(4)] for y in range(4) for k in range(2)]


def owner_groups():
    lines = [(zl + 4 * zh) for zl in range(4) for zh in range(2)]
    groups = [[device(x, y, z, 0) for y in range(4) for z in lines] for x in range(4)]
    return groups + [[device(x, y, z, 1) for x in range(4) for z in lines] for y in range(4)]


def shifted(step):
    pairs = []
    for i in range(256):
        x, zl, core, zh, y = i % 4, i // 4 % 4, i // 16 % 2, i // 32 % 2, i // 64
        z = zl + 4 * zh
        pairs.append((i, device(x, (y + step) % 4, z, 1) if core else device((x + step) % 4, y, z, 0)))
    return pairs


SWAP = [(i, i ^ 16) for i in range(256)]


def swap_cores(array):
    return lax.ppermute(array, AXES, SWAP)


def send(array, step):
    return lax.ppermute(array, AXES, shifted(step))


def exchange(array, groups):
    return lax.all_to_all(array, AXES, 0, 0, axis_index_groups=groups, tiled=True)


def sent_order(place, half):
    sent = lax.broadcasted_iota(jnp.int32, (ROWS, ROWS), 0)
    flat = lax.broadcasted_iota(jnp.int32, (ROWS, ROWS), 1)
    own, a_step = jnp.where(half == 0, place % 4, place // 64), jnp.where(half == 0, 8, 2)
    a, b = (sent // 32 + own) % 4, sent // 8 % 4
    return (sent // 2 % 4 * 32 + a * a_step + b * (10 - a_step) + sent % 2 == flat).astype(F32).astype(BF16)


def gathered_order(half):
    sent = lax.broadcasted_iota(jnp.int32, (ROWS, ROWS), 1)
    flat = lax.broadcasted_iota(jnp.int32, (ROWS, ROWS), 0)
    a, k, b, p = sent // 32, sent // 16 % 2, sent // 4 % 4, sent % 4
    z = (2 * p + k + half) % 8
    a_step = jnp.where(half == 0, 8, 2)
    return (z % 4 * 32 + a * a_step + b * (10 - a_step) + z // 4 == flat).astype(F32).astype(BF16)


def compensate_kernel(other, place_ref, codes_hbm, scales_hbm, feedback_hbm, out_ref, codes, scales, feedback, turned, spread, summed, sems):
    core = place_ref[0] // 16 % 2
    half = 1 - core if other else core
    copies = [pltpu.make_async_copy(scales_hbm, scales, sems.at[2 * CHUNKS])]
    for i in range(CHUNKS):
        columns = pl.ds(pl.multiple_of(half * HALF + i * CHUNK, LANES), CHUNK)
        copies.append(pltpu.make_async_copy(codes_hbm.at[:, columns], codes.at[i], sems.at[2 * i]))
        copies.append(pltpu.make_async_copy(feedback_hbm.at[:, columns], feedback.at[i], sems.at[2 * i + 1]))
    for copy in copies:
        copy.start()
    moved = sent_order(place_ref[0], half)
    copies[0].wait()
    turned[0:SLAB_ROWS, :] = scales[pl.ds(half * SLAB_ROWS, SLAB_ROWS), :]
    scale = turned[...].T
    for at in range(SLAB_ROWS):
        spread[:, at * LANES : (at + 1) * LANES] = jnp.broadcast_to(scale[:, at : at + 1], (ROWS, LANES))
    for i in range(CHUNKS):
        copies[1 + 2 * i].wait()
        copies[2 + 2 * i].wait()
        columns = slice(i * CHUNK, (i + 1) * CHUNK)
        dequant = codes[i].astype(F32) * spread[:, columns]
        summed[:, columns] = (dequant + feedback[i].astype(F32)).astype(BF16)
    for i in range(CHUNKS):
        columns = slice(i * CHUNK, (i + 1) * CHUNK)
        out_ref[:, columns] = jnp.dot(moved, summed[:, columns], preferred_element_type=F32).astype(BF16)


def compensate(other, place, codes, scales, feedback):
    return pl.pallas_call(
        functools.partial(compensate_kernel, other),
        out_shape=jax.ShapeDtypeStruct((ROWS, HALF), BF16),
        in_specs=[SCALAR, FAR, FAR, FAR],
        out_specs=WHOLE,
        scratch_shapes=[
            pltpu.VMEM((CHUNKS, ROWS, CHUNK), jnp.int32),
            pltpu.VMEM((WIDTH // LANES, ROWS), F32),
            pltpu.VMEM((CHUNKS, ROWS, CHUNK), BF16),
            pltpu.VMEM((ROWS, LANES), F32),
            pltpu.VMEM((ROWS, HALF), F32),
            pltpu.VMEM((ROWS, HALF), BF16),
            pltpu.SemaphoreType.DMA((2 * CHUNKS + 1,)),
        ],
        compiler_params=params(),
        cost_estimate=pl.CostEstimate(flops=2 * ROWS * ROWS * HALF, bytes_accessed=8 * ROWS * HALF, transcendentals=0),
        name="compensate",
    )(place, in_hbm(codes), in_hbm(scales), in_hbm(feedback))


def pair_sum_kernel(own_ref, other_ref, *out_refs):
    for piece, out_ref in enumerate(out_refs):
        rows = slice(piece * 32, (piece + 1) * 32)
        out_ref[...] = (own_ref[rows, :].astype(F32) + other_ref[rows, :].astype(F32)).astype(BF16)


def pair_sum(own, other):
    return pl.pallas_call(
        pair_sum_kernel,
        out_shape=[jax.ShapeDtypeStruct((32, HALF), BF16)] * 4,
        in_specs=[WHOLE] * 2,
        out_specs=[WHOLE] * 4,
        compiler_params=params(),
        name="pair_sum",
    )(own, other)


def line_sum_kernel(own_ref, a_ref, b_ref, c_ref, out_ref):
    total = own_ref[...].astype(F32) + a_ref[...].astype(F32) + b_ref[...].astype(F32) + c_ref[...].astype(F32)
    out_ref[...] = total.astype(BF16)


def line_sum(own, arrived):
    return pl.pallas_call(
        line_sum_kernel,
        out_shape=jax.ShapeDtypeStruct((32, HALF), BF16),
        in_specs=[WHOLE] * 4,
        out_specs=WHOLE,
        compiler_params=params(),
        name="line_sum",
    )(own, *arrived)


def adam_kernel(arrived_ref, master_ref, moment_ref, second_ref, dir_ref, new_ref, copies_ref):
    total = jnp.sum(arrived_ref[...].astype(F32), axis=0)
    grad = jnp.concatenate([total[0:1], total[1:2]], axis=1) / 256.0
    first = beta_one * moment_ref[...] + (1.0 - beta_one) * grad
    squared = beta_two * second_ref[...] + (1.0 - beta_two) * grad * grad
    first_hat = first / (1.0 - beta_one**adam_count)
    squared_hat = squared / (1.0 - beta_two**adam_count)
    adam_dir = first_hat / (jnp.sqrt(squared_hat) + adam_epsilon)
    new_master = master_ref[...] - learn_rate * adam_dir
    dir_ref[...] = adam_dir
    new_ref[...] = new_master
    rows = jnp.concatenate([new_master[:, : SLAB[1]], new_master[:, SLAB[1] :]], axis=0)
    copies_ref[...] = jnp.broadcast_to(rows.astype(BF16)[None], copies_ref.shape)


def adam(arrived, master, moment, second):
    slab = jax.ShapeDtypeStruct((1, HALF), F32)
    return pl.pallas_call(
        adam_kernel,
        out_shape=(slab, slab, jax.ShapeDtypeStruct((16, *SLAB), BF16)),
        in_specs=[WHOLE] * 4,
        out_specs=[WHOLE] * 3,
        compiler_params=params(),
        name="adam",
    )(arrived, master, moment, second)


def copies_kernel(in_ref, out_ref):
    out_ref[...] = jnp.broadcast_to(in_ref[...][None], out_ref.shape)


def copies_of(rows):
    return pl.pallas_call(
        copies_kernel,
        out_shape=jax.ShapeDtypeStruct((8, 16, HALF), BF16),
        in_specs=[WHOLE],
        out_specs=WHOLE,
        compiler_params=params(),
        name="copies_of",
    )(rows)


def place_half(half, rows_ref, weights_hbm, staged, sems):
    moved = gathered_order(half)
    copies = []
    for i in range(CHUNKS):
        rows = rows_ref[:, i * CHUNK : (i + 1) * CHUNK]
        staged[i] = jnp.dot(moved, rows, preferred_element_type=F32).astype(BF16)
        to = pl.ds(pl.multiple_of(half * HALF + i * CHUNK, LANES), CHUNK)
        copies.append(pltpu.make_async_copy(staged.at[i], weights_hbm.at[:, to], sems.at[i]))
        copies[-1].start()
    return copies


def restore_own_kernel(core_ref, rows_ref, dir_ref, new_ref, weights_hbm, dir_hbm, new_hbm, staged, sems):
    copies = [
        pltpu.make_async_copy(dir_ref, dir_hbm, sems.at[CHUNKS]),
        pltpu.make_async_copy(new_ref, new_hbm, sems.at[CHUNKS + 1]),
    ]
    for copy in copies:
        copy.start()
    for copy in copies + place_half(core_ref[0], rows_ref, weights_hbm, staged, sems):
        copy.wait()


def restore_own(core, rows, adam_dir, new_master):
    slab = jax.ShapeDtypeStruct((1, HALF), F32)
    return pl.pallas_call(
        restore_own_kernel,
        out_shape=(jax.ShapeDtypeStruct((ROWS, WIDTH), BF16), slab, slab),
        in_specs=[SCALAR] + [WHOLE] * 3,
        out_specs=[FAR] * 3,
        scratch_shapes=[pltpu.VMEM((CHUNKS, ROWS, CHUNK), BF16), pltpu.SemaphoreType.DMA((CHUNKS + 2,))],
        compiler_params=params(),
        name="restore_own",
    )(core, rows, adam_dir, new_master)


def restore_other_kernel(core_ref, rows_ref, held_hbm, weights_hbm, staged, sems):
    for copy in place_half(1 - core_ref[0], rows_ref, weights_hbm, staged, sems):
        copy.wait()


def restore_other(core, rows, weights):
    return pl.pallas_call(
        restore_other_kernel,
        out_shape=jax.ShapeDtypeStruct((ROWS, WIDTH), BF16),
        in_specs=[SCALAR, WHOLE, FAR],
        out_specs=FAR,
        scratch_shapes=[pltpu.VMEM((CHUNKS, ROWS, CHUNK), BF16), pltpu.SemaphoreType.DMA((CHUNKS,))],
        input_output_aliases={2: 0},
        compiler_params=params(),
        name="restore_other",
    )(core, rows, weights)


def shards(grad_codes, scales, feedback, master, moment, second):
    core = lax.axis_index("core").astype(jnp.int32).reshape(1)
    place = lax.axis_index(AXES).astype(jnp.int32).reshape(1)
    codes, feed = grad_codes[0, 0], feedback[0, 0]
    turned = jnp.swapaxes(scales[0, 0], 0, 1)
    given = compensate(True, place, codes, turned, feed)
    taken = swap_cores(given)
    kept = compensate(False, place, codes, turned, feed)
    own, *others = pair_sum(kept, taken)
    partial = line_sum(own, [send(others[step - 1], step) for step in (2, 1, 3)])
    arrived = exchange(partial.reshape(32, *SLAB), owner_groups())
    adam_dir, new_master, copies = adam(arrived, master[0], moment[0], second[0])
    rows = exchange(copies, small_groups()).reshape(16, HALF)
    mine = exchange(copies_of(rows), large_groups()).reshape(ROWS, HALF)
    theirs = swap_cores(mine)
    weights, adam_dir, new_master = restore_own(core, mine, adam_dir, new_master)
    weights = restore_other(core, theirs, weights)
    return adam_dir[None], new_master[None], weights


def solution(mesh):
    fine = Mesh(mesh.devices.reshape(SIZES), AXES)
    wide, node = ("y", "zh", "core"), ("zl", "x")
    placed = (
        P(wide, node, None, None),
        P(wide, node, None, None),
        P(wide, node, None, None),
        P(node, wide, None),
        P(node, wide, None),
        P(node, wide, None),
    )
    return jax.shard_map(
        shards,
        mesh=fine,
        in_specs=placed,
        out_specs=(P(node, wide, None), P(node, wide, None), P()),
        check_vma=False,
    )
```

```python
import functools

import jax
import jax.numpy as jnp
from jax import lax
from jax.experimental import pallas as pl
from jax.experimental.pallas import tpu as pltpu
from jax.sharding import Mesh
from jax.sharding import PartitionSpec as P

beta_one = 0.9
beta_two = 0.999
adam_count = 100.0
adam_epsilon = 1e-08
learn_rate = 0.02

AXES = ("y", "zh", "core", "zl", "x")
SIZES = (4, 2, 2, 4, 4)
ROWS = 128
WIDTH = 9216
HALF = WIDTH // 2
LANES = 128
CHUNKS = 3
CHUNK = HALF // CHUNKS
PER_CHUNK = CHUNK // LANES
SLAB_ROWS = HALF // LANES
SLAB = (2, HALF // 2)
F32 = jnp.float32
BF16 = jnp.bfloat16
VMEM_LIMIT = 32 * 1024 * 1024
WHOLE = pl.BlockSpec(memory_space=pltpu.VMEM)
SCALAR = pl.BlockSpec(memory_space=pltpu.SMEM)
FAR = pl.BlockSpec(memory_space=pltpu.HBM)


def params():
    return pltpu.CompilerParams(vmem_limit_bytes=VMEM_LIMIT)


def in_hbm(array):
    return pltpu.with_memory_space_constraint(array, pltpu.HBM)


def device(x, y, z, core):
    return (((y * 2 + z // 4) * 2 + core) * 4 + z % 4) * 4 + x


def owner_groups():
    lines = [(zl + 4 * zh) for zl in range(4) for zh in range(2)]
    groups = [[device(x, y, z, 0) for y in range(4) for z in lines] for x in range(4)]
    return groups + [[device(x, y, z, 1) for x in range(4) for z in lines] for y in range(4)]


def shifted(step):
    pairs = []
    for i in range(256):
        x, zl, core, zh, y = i % 4, i // 4 % 4, i // 16 % 2, i // 32 % 2, i // 64
        z = zl + 4 * zh
        pairs.append((i, device(x, (y + step) % 4, z, 1) if core else device((x + step) % 4, y, z, 0)))
    return pairs


SWAP = [(i, i ^ 16) for i in range(256)]


def swap_cores(array):
    return lax.ppermute(array, AXES, SWAP)


def send(array, step):
    return lax.ppermute(array, AXES, shifted(step))


def exchange(array, groups):
    return lax.all_to_all(array, AXES, 0, 0, axis_index_groups=groups, tiled=True)


def order(place, half, transposed):
    sent = lax.broadcasted_iota(jnp.int32, (ROWS, ROWS), 1 if transposed else 0)
    flat = lax.broadcasted_iota(jnp.int32, (ROWS, ROWS), 0 if transposed else 1)
    own, a_step = jnp.where(half == 0, place % 4, place // 64), jnp.where(half == 0, 8, 2)
    a, b = (sent // 32 + own) % 4, sent // 8 % 4
    return (sent // 2 % 4 * 32 + a * a_step + b * (10 - a_step) + sent % 2 == flat).astype(F32).astype(BF16)


def compensate_kernel(other, place_ref, codes_hbm, scales_hbm, feedback_hbm, out_ref, codes, scales, feedback, turned, spread, summed, sems):
    core = place_ref[0] // 16 % 2
    half = 1 - core if other else core
    copies = [pltpu.make_async_copy(scales_hbm, scales, sems.at[2 * CHUNKS])]
    for i in range(CHUNKS):
        columns = pl.ds(pl.multiple_of(half * HALF + i * CHUNK, LANES), CHUNK)
        copies.append(pltpu.make_async_copy(codes_hbm.at[:, columns], codes.at[i], sems.at[2 * i]))
        copies.append(pltpu.make_async_copy(feedback_hbm.at[:, columns], feedback.at[i], sems.at[2 * i + 1]))
    for copy in copies:
        copy.start()
    moved = order(place_ref[0], half, False)
    copies[0].wait()
    turned[0:SLAB_ROWS, :] = scales[pl.ds(half * SLAB_ROWS, SLAB_ROWS), :]
    scale = turned[...].T
    for at in range(SLAB_ROWS):
        spread[:, at * LANES : (at + 1) * LANES] = jnp.broadcast_to(scale[:, at : at + 1], (ROWS, LANES))
    for i in range(CHUNKS):
        copies[1 + 2 * i].wait()
        copies[2 + 2 * i].wait()
        columns = slice(i * CHUNK, (i + 1) * CHUNK)
        dequant = codes[i].astype(F32) * spread[:, columns]
        summed[:, columns] = (dequant + feedback[i].astype(F32)).astype(BF16)
    for i in range(CHUNKS):
        columns = slice(i * CHUNK, (i + 1) * CHUNK)
        out_ref[:, columns] = jnp.dot(moved, summed[:, columns], preferred_element_type=F32).astype(BF16)


def compensate(other, place, codes, scales, feedback):
    return pl.pallas_call(
        functools.partial(compensate_kernel, other),
        out_shape=jax.ShapeDtypeStruct((ROWS, HALF), BF16),
        in_specs=[SCALAR, FAR, FAR, FAR],
        out_specs=WHOLE,
        scratch_shapes=[
            pltpu.VMEM((CHUNKS, ROWS, CHUNK), jnp.int32),
            pltpu.VMEM((WIDTH // LANES, ROWS), F32),
            pltpu.VMEM((CHUNKS, ROWS, CHUNK), BF16),
            pltpu.VMEM((ROWS, LANES), F32),
            pltpu.VMEM((ROWS, HALF), F32),
            pltpu.VMEM((ROWS, HALF), BF16),
            pltpu.SemaphoreType.DMA((2 * CHUNKS + 1,)),
        ],
        compiler_params=params(),
        cost_estimate=pl.CostEstimate(flops=2 * ROWS * ROWS * HALF, bytes_accessed=8 * ROWS * HALF, transcendentals=0),
        name="compensate",
    )(place, in_hbm(codes), in_hbm(scales), in_hbm(feedback))


def pair_sum_kernel(own_ref, other_ref, *out_refs):
    for piece, out_ref in enumerate(out_refs):
        rows = slice(piece * 32, (piece + 1) * 32)
        out_ref[...] = (own_ref[rows, :].astype(F32) + other_ref[rows, :].astype(F32)).astype(BF16)


def pair_sum(own, other):
    return pl.pallas_call(
        pair_sum_kernel,
        out_shape=[jax.ShapeDtypeStruct((32, HALF), BF16)] * 4,
        in_specs=[WHOLE] * 2,
        out_specs=[WHOLE] * 4,
        compiler_params=params(),
        name="pair_sum",
    )(own, other)


def line_sum_kernel(own_ref, a_ref, b_ref, c_ref, out_ref):
    total = own_ref[...].astype(F32) + a_ref[...].astype(F32) + b_ref[...].astype(F32) + c_ref[...].astype(F32)
    out_ref[...] = total.astype(BF16)


def line_sum(own, arrived):
    return pl.pallas_call(
        line_sum_kernel,
        out_shape=jax.ShapeDtypeStruct((32, HALF), BF16),
        in_specs=[WHOLE] * 4,
        out_specs=WHOLE,
        compiler_params=params(),
        name="line_sum",
    )(own, *arrived)


def adam_kernel(arrived_ref, master_ref, moment_ref, second_ref, dir_ref, new_ref, copies_ref):
    total = jnp.sum(arrived_ref[...].astype(F32), axis=0)
    grad = jnp.concatenate([total[0:1], total[1:2]], axis=1) / 256.0
    first = beta_one * moment_ref[...] + (1.0 - beta_one) * grad
    squared = beta_two * second_ref[...] + (1.0 - beta_two) * grad * grad
    first_hat = first / (1.0 - beta_one**adam_count)
    squared_hat = squared / (1.0 - beta_two**adam_count)
    adam_dir = first_hat / (jnp.sqrt(squared_hat) + adam_epsilon)
    new_master = master_ref[...] - learn_rate * adam_dir
    dir_ref[...] = adam_dir
    new_ref[...] = new_master
    rows = jnp.concatenate([new_master[:, : SLAB[1]], new_master[:, SLAB[1] :]], axis=0)
    copies_ref[...] = jnp.broadcast_to(rows.astype(BF16)[None], copies_ref.shape)


def adam(arrived, master, moment, second):
    slab = jax.ShapeDtypeStruct((1, HALF), F32)
    return pl.pallas_call(
        adam_kernel,
        out_shape=(slab, slab, jax.ShapeDtypeStruct((32, *SLAB), BF16)),
        in_specs=[WHOLE] * 4,
        out_specs=[WHOLE] * 3,
        compiler_params=params(),
        name="adam",
    )(arrived, master, moment, second)


def place_half(place, half, blocks, weights_hbm, staged, sems):
    moved = order(place, half, True)
    copies = []
    for i in range(CHUNKS):
        rows = jnp.concatenate([block[:, i * CHUNK : (i + 1) * CHUNK] for block in blocks], axis=0)
        staged[i] = jnp.dot(moved, rows, preferred_element_type=F32).astype(BF16)
        to = pl.ds(pl.multiple_of(half * HALF + i * CHUNK, LANES), CHUNK)
        copies.append(pltpu.make_async_copy(staged.at[i], weights_hbm.at[:, to], sems.at[i]))
        copies[-1].start()
    return copies


def restore_own_kernel(place_ref, a_ref, b_ref, c_ref, d_ref, dir_ref, new_ref, weights_hbm, dir_hbm, new_hbm, staged, sems):
    copies = [
        pltpu.make_async_copy(dir_ref, dir_hbm, sems.at[CHUNKS]),
        pltpu.make_async_copy(new_ref, new_hbm, sems.at[CHUNKS + 1]),
    ]
    for copy in copies:
        copy.start()
    half = place_ref[0] // 16 % 2
    for copy in copies + place_half(place_ref[0], half, (a_ref, b_ref, c_ref, d_ref), weights_hbm, staged, sems):
        copy.wait()


def restore_own(place, blocks, adam_dir, new_master):
    slab = jax.ShapeDtypeStruct((1, HALF), F32)
    return pl.pallas_call(
        restore_own_kernel,
        out_shape=(jax.ShapeDtypeStruct((ROWS, WIDTH), BF16), slab, slab),
        in_specs=[SCALAR] + [WHOLE] * 6,
        out_specs=[FAR] * 3,
        scratch_shapes=[pltpu.VMEM((CHUNKS, ROWS, CHUNK), BF16), pltpu.SemaphoreType.DMA((CHUNKS + 2,))],
        compiler_params=params(),
        name="restore_own",
    )(place, *blocks, adam_dir, new_master)


def restore_other_kernel(place_ref, a_ref, b_ref, c_ref, d_ref, held_hbm, weights_hbm, staged, sems):
    half = 1 - place_ref[0] // 16 % 2
    for copy in place_half(place_ref[0], half, (a_ref, b_ref, c_ref, d_ref), weights_hbm, staged, sems):
        copy.wait()


def restore_other(place, blocks, weights):
    return pl.pallas_call(
        restore_other_kernel,
        out_shape=jax.ShapeDtypeStruct((ROWS, WIDTH), BF16),
        in_specs=[SCALAR] + [WHOLE] * 4 + [FAR],
        out_specs=FAR,
        scratch_shapes=[pltpu.VMEM((CHUNKS, ROWS, CHUNK), BF16), pltpu.SemaphoreType.DMA((CHUNKS,))],
        input_output_aliases={5: 0},
        compiler_params=params(),
        name="restore_other",
    )(place, *blocks, weights)


def shards(grad_codes, scales, feedback, master, moment, second):
    place = lax.axis_index(AXES).astype(jnp.int32).reshape(1)
    codes, feed = grad_codes[0, 0], feedback[0, 0]
    turned = jnp.swapaxes(scales[0, 0], 0, 1)
    given = compensate(True, place, codes, turned, feed)
    taken = swap_cores(given)
    kept = compensate(False, place, codes, turned, feed)
    own, *others = pair_sum(kept, taken)
    partial = line_sum(own, [send(others[step - 1], step) for step in (2, 1, 3)])
    arrived = exchange(partial.reshape(32, *SLAB), owner_groups())
    adam_dir, new_master, copies = adam(arrived, master[0], moment[0], second[0])
    joined = exchange(copies, owner_groups()).reshape(32, HALF)
    across, after, before = [send(joined, 4 - step) for step in (2, 1, 3)]
    mine = [joined, after, across, before]
    theirs = [swap_cores(block) for block in mine]
    weights, adam_dir, new_master = restore_own(place, mine, adam_dir, new_master)
    weights = restore_other(place, theirs, weights)
    return adam_dir[None], new_master[None], weights


def solution(mesh):
    fine = Mesh(mesh.devices.reshape(SIZES), AXES)
    wide, node = ("y", "zh", "core"), ("zl", "x")
    placed = (
        P(wide, node, None, None),
        P(wide, node, None, None),
        P(wide, node, None, None),
        P(node, wide, None),
        P(node, wide, None),
        P(node, wide, None),
    )
    return jax.shard_map(
        shards,
        mesh=fine,
        in_specs=placed,
        out_specs=(P(node, wide, None), P(node, wide, None), P()),
        check_vma=False,
    )
```

```python
import functools

import jax
import jax.numpy as jnp
from jax import lax
from jax.experimental import pallas as pl
from jax.experimental.pallas import tpu as pltpu
from jax.sharding import Mesh
from jax.sharding import PartitionSpec as P

beta_one = 0.9
beta_two = 0.999
adam_count = 100.0
adam_epsilon = 1e-08
learn_rate = 0.02

AXES = ("y", "zh", "core", "zl", "x")
SIZES = (4, 2, 2, 4, 4)
ROWS = 128
WIDTH = 9216
HALF = WIDTH // 2
LANES = 128
CHUNKS = 3
CHUNK = HALF // CHUNKS
PER_CHUNK = CHUNK // LANES
SLAB_ROWS = HALF // LANES
SLAB = (2, HALF // 2)
F32 = jnp.float32
BF16 = jnp.bfloat16
VMEM_LIMIT = 32 * 1024 * 1024
WHOLE = pl.BlockSpec(memory_space=pltpu.VMEM)
SCALAR = pl.BlockSpec(memory_space=pltpu.SMEM)
FAR = pl.BlockSpec(memory_space=pltpu.HBM)


def params():
    return pltpu.CompilerParams(vmem_limit_bytes=VMEM_LIMIT)


def in_hbm(array):
    return pltpu.with_memory_space_constraint(array, pltpu.HBM)


def device(x, y, z, core):
    return (((y * 2 + z // 4) * 2 + core) * 4 + z % 4) * 4 + x


def owner_groups():
    lines = [(zl + 4 * zh) for zl in range(4) for zh in range(2)]
    groups = [[device(x, y, z, 0) for y in range(4) for z in lines] for x in range(4)]
    return groups + [[device(x, y, z, 1) for x in range(4) for z in lines] for y in range(4)]


def shifted(step):
    pairs = []
    for i in range(256):
        x, zl, core, zh, y = i % 4, i // 4 % 4, i // 16 % 2, i // 32 % 2, i // 64
        z = zl + 4 * zh
        pairs.append((i, device(x, (y + step) % 4, z, 1) if core else device((x + step) % 4, y, z, 0)))
    return pairs


SWAP = [(i, i ^ 16) for i in range(256)]


def swap_cores(array):
    return lax.ppermute(array, AXES, SWAP)


def send(array, step):
    return lax.ppermute(array, AXES, shifted(step))


def exchange(array, groups):
    return lax.all_to_all(array, AXES, 0, 0, axis_index_groups=groups, tiled=True)


def order(place, half, transposed):
    sent = lax.broadcasted_iota(jnp.int32, (ROWS, ROWS), 1 if transposed else 0)
    flat = lax.broadcasted_iota(jnp.int32, (ROWS, ROWS), 0 if transposed else 1)
    own, a_step = jnp.where(half == 0, place % 4, place // 64), jnp.where(half == 0, 8, 2)
    a, b = (sent // 32 + own) % 4, sent // 8 % 4
    return (sent // 2 % 4 * 32 + a * a_step + b * (10 - a_step) + sent % 2 == flat).astype(F32).astype(BF16)


def compensate_kernel(other, place_ref, codes_hbm, scales_hbm, feedback_hbm, out_ref, codes, scales, feedback, turned, spread, summed, sems):
    core = place_ref[0] // 16 % 2
    half = 1 - core if other else core
    copies = [pltpu.make_async_copy(scales_hbm, scales, sems.at[2 * CHUNKS])]
    for i in range(CHUNKS):
        columns = pl.ds(pl.multiple_of(half * HALF + i * CHUNK, LANES), CHUNK)
        copies.append(pltpu.make_async_copy(codes_hbm.at[:, columns], codes.at[i], sems.at[2 * i]))
        copies.append(pltpu.make_async_copy(feedback_hbm.at[:, columns], feedback.at[i], sems.at[2 * i + 1]))
    for copy in copies:
        copy.start()
    moved = order(place_ref[0], half, False)
    copies[0].wait()
    turned[0:SLAB_ROWS, :] = scales[pl.ds(half * SLAB_ROWS, SLAB_ROWS), :]
    scale = turned[...].T
    for at in range(SLAB_ROWS):
        spread[:, at * LANES : (at + 1) * LANES] = jnp.broadcast_to(scale[:, at : at + 1], (ROWS, LANES))
    for i in range(CHUNKS):
        copies[1 + 2 * i].wait()
        copies[2 + 2 * i].wait()
        columns = slice(i * CHUNK, (i + 1) * CHUNK)
        dequant = codes[i].astype(F32) * spread[:, columns]
        summed[:, columns] = (dequant + feedback[i].astype(F32)).astype(BF16)
    for i in range(CHUNKS):
        columns = slice(i * CHUNK, (i + 1) * CHUNK)
        out_ref[:, columns] = jnp.dot(moved, summed[:, columns], preferred_element_type=F32).astype(BF16)


def compensate(other, place, codes, scales, feedback):
    return pl.pallas_call(
        functools.partial(compensate_kernel, other),
        out_shape=jax.ShapeDtypeStruct((ROWS, HALF), BF16),
        in_specs=[SCALAR, FAR, FAR, FAR],
        out_specs=WHOLE,
        scratch_shapes=[
            pltpu.VMEM((CHUNKS, ROWS, CHUNK), jnp.int32),
            pltpu.VMEM((WIDTH // LANES, ROWS), F32),
            pltpu.VMEM((CHUNKS, ROWS, CHUNK), BF16),
            pltpu.VMEM((ROWS, LANES), F32),
            pltpu.VMEM((ROWS, HALF), F32),
            pltpu.VMEM((ROWS, HALF), BF16),
            pltpu.SemaphoreType.DMA((2 * CHUNKS + 1,)),
        ],
        compiler_params=params(),
        cost_estimate=pl.CostEstimate(flops=2 * ROWS * ROWS * HALF, bytes_accessed=8 * ROWS * HALF, transcendentals=0),
        name="compensate",
    )(place, in_hbm(codes), in_hbm(scales), in_hbm(feedback))


def pair_sum_kernel(own_ref, other_ref, *out_refs):
    for piece, out_ref in enumerate(out_refs):
        rows = slice(piece * 32, (piece + 1) * 32)
        out_ref[...] = (own_ref[rows, :].astype(F32) + other_ref[rows, :].astype(F32)).astype(BF16)


def pair_sum(own, other):
    return pl.pallas_call(
        pair_sum_kernel,
        out_shape=[jax.ShapeDtypeStruct((32, HALF), BF16)] * 4,
        in_specs=[WHOLE] * 2,
        out_specs=[WHOLE] * 4,
        compiler_params=params(),
        name="pair_sum",
    )(own, other)


def line_sum_kernel(own_ref, a_ref, b_ref, c_ref, out_ref):
    total = own_ref[...].astype(F32) + a_ref[...].astype(F32) + b_ref[...].astype(F32) + c_ref[...].astype(F32)
    out_ref[...] = total.astype(BF16)


def line_sum(own, arrived):
    return pl.pallas_call(
        line_sum_kernel,
        out_shape=jax.ShapeDtypeStruct((32, HALF), BF16),
        in_specs=[WHOLE] * 4,
        out_specs=WHOLE,
        compiler_params=params(),
        name="line_sum",
    )(own, *arrived)


def adam_kernel(arrived_ref, master_ref, moment_ref, second_ref, dir_ref, new_ref, copies_ref):
    total = arrived_ref[0].astype(F32)
    for piece in range(1, 32):
        total = total + arrived_ref[piece].astype(F32)
    grad = jnp.concatenate([total[0:1], total[1:2]], axis=1) / 256.0
    first = beta_one * moment_ref[...] + (1.0 - beta_one) * grad
    squared = beta_two * second_ref[...] + (1.0 - beta_two) * grad * grad
    first_hat = first / (1.0 - beta_one**adam_count)
    squared_hat = squared / (1.0 - beta_two**adam_count)
    adam_dir = first_hat / (jnp.sqrt(squared_hat) + adam_epsilon)
    new_master = master_ref[...] - learn_rate * adam_dir
    dir_ref[...] = adam_dir
    new_ref[...] = new_master
    rows = jnp.concatenate([new_master[:, : SLAB[1]], new_master[:, SLAB[1] :]], axis=0)
    copies_ref[...] = jnp.broadcast_to(rows.astype(BF16)[None], copies_ref.shape)


def adam(arrived, master, moment, second):
    slab = jax.ShapeDtypeStruct((1, HALF), F32)
    return pl.pallas_call(
        adam_kernel,
        out_shape=(slab, slab, jax.ShapeDtypeStruct((32, *SLAB), BF16)),
        in_specs=[WHOLE] * 4,
        out_specs=[WHOLE] * 3,
        compiler_params=params(),
        name="adam",
    )(arrived, master, moment, second)


def place_half(place, half, blocks, weights_hbm, staged, sems):
    own, across, after, before = blocks
    moved = order(place, half, True)
    copies = []
    for i in range(CHUNKS):
        rows = jnp.concatenate([block[:, i * CHUNK : (i + 1) * CHUNK] for block in (own, after, across, before)], axis=0)
        staged[i] = jnp.dot(moved, rows, preferred_element_type=F32).astype(BF16)
        to = pl.ds(pl.multiple_of(half * HALF + i * CHUNK, LANES), CHUNK)
        copies.append(pltpu.make_async_copy(staged.at[i], weights_hbm.at[:, to], sems.at[i]))
        copies[-1].start()
    return copies


def restore_own_kernel(place_ref, a_ref, b_ref, c_ref, d_ref, dir_ref, new_ref, weights_hbm, dir_hbm, new_hbm, staged, sems):
    copies = [
        pltpu.make_async_copy(dir_ref, dir_hbm, sems.at[CHUNKS]),
        pltpu.make_async_copy(new_ref, new_hbm, sems.at[CHUNKS + 1]),
    ]
    for copy in copies:
        copy.start()
    half = place_ref[0] // 16 % 2
    for copy in copies + place_half(place_ref[0], half, (a_ref, b_ref, c_ref, d_ref), weights_hbm, staged, sems):
        copy.wait()


def restore_own(place, blocks, adam_dir, new_master):
    slab = jax.ShapeDtypeStruct((1, HALF), F32)
    return pl.pallas_call(
        restore_own_kernel,
        out_shape=(jax.ShapeDtypeStruct((ROWS, WIDTH), BF16), slab, slab),
        in_specs=[SCALAR] + [WHOLE] * 6,
        out_specs=[FAR] * 3,
        scratch_shapes=[pltpu.VMEM((CHUNKS, ROWS, CHUNK), BF16), pltpu.SemaphoreType.DMA((CHUNKS + 2,))],
        compiler_params=params(),
        name="restore_own",
    )(place, *blocks, adam_dir, new_master)


def restore_other_kernel(place_ref, a_ref, b_ref, c_ref, d_ref, held_hbm, weights_hbm, staged, sems):
    half = 1 - place_ref[0] // 16 % 2
    for copy in place_half(place_ref[0], half, (a_ref, b_ref, c_ref, d_ref), weights_hbm, staged, sems):
        copy.wait()


def restore_other(place, blocks, weights):
    return pl.pallas_call(
        restore_other_kernel,
        out_shape=jax.ShapeDtypeStruct((ROWS, WIDTH), BF16),
        in_specs=[SCALAR] + [WHOLE] * 4 + [FAR],
        out_specs=FAR,
        scratch_shapes=[pltpu.VMEM((CHUNKS, ROWS, CHUNK), BF16), pltpu.SemaphoreType.DMA((CHUNKS,))],
        input_output_aliases={5: 0},
        compiler_params=params(),
        name="restore_other",
    )(place, *blocks, weights)


def shards(grad_codes, scales, feedback, master, moment, second):
    place = lax.axis_index(AXES).astype(jnp.int32).reshape(1)
    codes, feed = grad_codes[0, 0], feedback[0, 0]
    turned = jnp.swapaxes(scales[0, 0], 0, 1)
    given = compensate(True, place, codes, turned, feed)
    taken = swap_cores(given)
    kept = compensate(False, place, codes, turned, feed)
    own, *others = pair_sum(kept, taken)
    partial = line_sum(own, [send(others[step - 1], step) for step in (2, 1, 3)])
    arrived = exchange(partial.reshape(32, *SLAB), owner_groups())
    adam_dir, new_master, copies = adam(arrived, master[0], moment[0], second[0])
    joined = exchange(copies, owner_groups()).reshape(32, HALF)
    across, after, before = [send(joined, 4 - step) for step in (2, 1, 3)]
    mine = [joined, across, after, before]
    theirs = [swap_cores(block) for block in mine]
    weights, adam_dir, new_master = restore_own(place, mine, adam_dir, new_master)
    weights = restore_other(place, theirs, weights)
    return adam_dir[None], new_master[None], weights


def solution(mesh):
    fine = Mesh(mesh.devices.reshape(SIZES), AXES)
    wide, node = ("y", "zh", "core"), ("zl", "x")
    placed = (
        P(wide, node, None, None),
        P(wide, node, None, None),
        P(wide, node, None, None),
        P(node, wide, None),
        P(node, wide, None),
        P(node, wide, None),
    )
    return jax.shard_map(
        shards,
        mesh=fine,
        in_specs=placed,
        out_specs=(P(node, wide, None), P(node, wide, None), P()),
        check_vma=False,
    )
```

```python
import functools

import jax
import jax.numpy as jnp
from jax import lax
from jax.experimental import pallas as pl
from jax.experimental.pallas import tpu as pltpu
from jax.sharding import Mesh
from jax.sharding import PartitionSpec as P

beta_one = 0.9
beta_two = 0.999
adam_count = 100.0
adam_epsilon = 1e-08
learn_rate = 0.02

AXES = ("y", "zh", "core", "zl", "x")
SIZES = (4, 2, 2, 4, 4)
ROWS = 128
WIDTH = 9216
HALF = WIDTH // 2
LANES = 128
CHUNKS = 3
CHUNK = HALF // CHUNKS
PER_CHUNK = CHUNK // LANES
SLAB_ROWS = HALF // LANES
SLAB = (2, HALF // 2)
F32 = jnp.float32
BF16 = jnp.bfloat16
VMEM_LIMIT = 32 * 1024 * 1024
WHOLE = pl.BlockSpec(memory_space=pltpu.VMEM)
SCALAR = pl.BlockSpec(memory_space=pltpu.SMEM)
FAR = pl.BlockSpec(memory_space=pltpu.HBM)


def params():
    return pltpu.CompilerParams(vmem_limit_bytes=VMEM_LIMIT)


def in_hbm(array):
    return pltpu.with_memory_space_constraint(array, pltpu.HBM)


def device(x, y, z, core):
    return (((y * 2 + z // 4) * 2 + core) * 4 + z % 4) * 4 + x


def owner_groups():
    lines = [(zl + 4 * zh) for zl in range(4) for zh in range(2)]
    groups = [[device(x, y, z, 0) for y in range(4) for z in lines] for x in range(4)]
    return groups + [[device(x, y, z, 1) for x in range(4) for z in lines] for y in range(4)]


def shifted(step):
    pairs = []
    for i in range(256):
        x, zl, core, zh, y = i % 4, i // 4 % 4, i // 16 % 2, i // 32 % 2, i // 64
        z = zl + 4 * zh
        pairs.append((i, device(x, (y + step) % 4, z, 1) if core else device((x + step) % 4, y, z, 0)))
    return pairs


SWAP = [(i, i ^ 16) for i in range(256)]


def swap_cores(array):
    return lax.ppermute(array, AXES, SWAP)


def send(array, step):
    return lax.ppermute(array, AXES, shifted(step))


def exchange(array, groups):
    return lax.all_to_all(array, AXES, 0, 0, axis_index_groups=groups, tiled=True)


def order(place, half, transposed):
    sent = lax.broadcasted_iota(jnp.int32, (ROWS, ROWS), 1 if transposed else 0)
    flat = lax.broadcasted_iota(jnp.int32, (ROWS, ROWS), 0 if transposed else 1)
    own, a_step = jnp.where(half == 0, place % 4, place // 64), jnp.where(half == 0, 8, 2)
    a, b = (sent // 32 + own) % 4, sent // 8 % 4
    return (sent // 2 % 4 * 32 + a * a_step + b * (10 - a_step) + sent % 2 == flat).astype(F32).astype(BF16)


def compensate_kernel(place_ref, codes_hbm, scales_hbm, feedback_hbm, *refs):
    *given_refs, kept_ref, codes, scales, feedback, turned, summed, sems = refs
    core = place_ref[0] // 16 % 2
    copies = [pltpu.make_async_copy(scales_hbm, scales, sems.at[4 * CHUNKS])]
    for turn in range(2):
        start = (core if turn else 1 - core) * HALF
        for i in range(CHUNKS):
            columns = pl.ds(pl.multiple_of(start + i * CHUNK, LANES), CHUNK)
            at = turn * CHUNKS + i
            copies.append(pltpu.make_async_copy(codes_hbm.at[:, columns], codes.at[at], sems.at[2 * at]))
            copies.append(pltpu.make_async_copy(feedback_hbm.at[:, columns], feedback.at[at], sems.at[2 * at + 1]))
    for copy in copies:
        copy.start()
    moved = [order(place_ref[0], 1 - core, False), order(place_ref[0], core, False)]
    copies[0].wait()
    for turn in range(2):
        half = core if turn else 1 - core
        turned[turn, 0:SLAB_ROWS, :] = scales[pl.ds(half * SLAB_ROWS, SLAB_ROWS), :]
        scale = turned[turn].T
        for i in range(CHUNKS):
            at = turn * CHUNKS + i
            copies[1 + 2 * at].wait()
            copies[2 + 2 * at].wait()
            for block in range(PER_CHUNK):
                columns = slice(block * LANES, (block + 1) * LANES)
                place = i * PER_CHUNK + block
                dequant = codes[at, :, columns].astype(F32) * scale[:, place : place + 1]
                into = slice(place * LANES, (place + 1) * LANES)
                summed[turn, :, into] = (dequant + feedback[at, :, columns].astype(F32)).astype(BF16)
        for i in range(CHUNKS):
            columns = slice(i * CHUNK, (i + 1) * CHUNK)
            rows = jnp.dot(moved[turn], summed[turn, :, columns], preferred_element_type=F32).astype(BF16)
            if turn:
                kept_ref[:, columns] = rows
            else:
                for piece, given_ref in enumerate(given_refs):
                    given_ref[:, columns] = rows[piece * 32 : (piece + 1) * 32]


def compensate(place, codes, scales, feedback):
    return pl.pallas_call(
        compensate_kernel,
        out_shape=[jax.ShapeDtypeStruct((32, HALF), BF16)] * 4 + [jax.ShapeDtypeStruct((ROWS, HALF), BF16)],
        in_specs=[SCALAR, FAR, FAR, FAR],
        out_specs=[WHOLE] * 5,
        scratch_shapes=[
            pltpu.VMEM((2 * CHUNKS, ROWS, CHUNK), jnp.int32),
            pltpu.VMEM((WIDTH // LANES, ROWS), F32),
            pltpu.VMEM((2 * CHUNKS, ROWS, CHUNK), BF16),
            pltpu.VMEM((2, ROWS, LANES), F32),
            pltpu.VMEM((2, ROWS, HALF), BF16),
            pltpu.SemaphoreType.DMA((4 * CHUNKS + 1,)),
        ],
        compiler_params=params(),
        name="compensate",
    )(place, in_hbm(codes), in_hbm(scales), in_hbm(feedback))


def pair_sum_kernel(piece, own_ref, other_ref, out_ref):
    own = own_ref[piece * 32 : (piece + 1) * 32, :].astype(F32)
    out_ref[...] = (own + other_ref[...].astype(F32)).astype(BF16)


def pair_sum(piece, own, other):
    return pl.pallas_call(
        functools.partial(pair_sum_kernel, piece),
        out_shape=jax.ShapeDtypeStruct((32, HALF), BF16),
        in_specs=[WHOLE] * 2,
        out_specs=WHOLE,
        compiler_params=params(),
        name="pair_sum",
    )(own, other)


def line_sum_kernel(own_ref, a_ref, b_ref, c_ref, out_ref):
    total = own_ref[...].astype(F32) + a_ref[...].astype(F32) + b_ref[...].astype(F32) + c_ref[...].astype(F32)
    out_ref[...] = total.astype(BF16)


def line_sum(own, arrived):
    return pl.pallas_call(
        line_sum_kernel,
        out_shape=jax.ShapeDtypeStruct((32, HALF), BF16),
        in_specs=[WHOLE] * 4,
        out_specs=WHOLE,
        compiler_params=params(),
        name="line_sum",
    )(own, *arrived)


def adam_kernel(arrived_ref, master_ref, moment_ref, second_ref, dir_ref, new_ref, copies_ref):
    total = arrived_ref[0].astype(F32)
    for piece in range(1, 32):
        total = total + arrived_ref[piece].astype(F32)
    grad = jnp.concatenate([total[0:1], total[1:2]], axis=1) / 256.0
    first = beta_one * moment_ref[...] + (1.0 - beta_one) * grad
    squared = beta_two * second_ref[...] + (1.0 - beta_two) * grad * grad
    first_hat = first / (1.0 - beta_one**adam_count)
    squared_hat = squared / (1.0 - beta_two**adam_count)
    adam_dir = first_hat / (jnp.sqrt(squared_hat) + adam_epsilon)
    new_master = master_ref[...] - learn_rate * adam_dir
    dir_ref[...] = adam_dir
    new_ref[...] = new_master
    rows = jnp.concatenate([new_master[:, : SLAB[1]], new_master[:, SLAB[1] :]], axis=0)
    copies_ref[...] = jnp.broadcast_to(rows.astype(BF16)[None], copies_ref.shape)


def adam(arrived, master, moment, second):
    slab = jax.ShapeDtypeStruct((1, HALF), F32)
    return pl.pallas_call(
        adam_kernel,
        out_shape=(slab, slab, jax.ShapeDtypeStruct((32, *SLAB), BF16)),
        in_specs=[WHOLE] * 4,
        out_specs=[WHOLE] * 3,
        compiler_params=params(),
        name="adam",
    )(arrived, master, moment, second)


def place_half(place, half, blocks, weights_hbm, staged, sems):
    moved = order(place, half, True)
    ordered = [blocks[i] for i in (0, 1, 3, 2)]
    copies = []
    for i in range(CHUNKS):
        rows = jnp.concatenate([block[:, i * CHUNK : (i + 1) * CHUNK] for block in ordered], axis=0)
        staged[i] = jnp.dot(moved, rows, preferred_element_type=F32).astype(BF16)
        to = pl.ds(pl.multiple_of(half * HALF + i * CHUNK, LANES), CHUNK)
        copies.append(pltpu.make_async_copy(staged.at[i], weights_hbm.at[:, to], sems.at[i]))
        copies[-1].start()
    return copies


def restore_own_kernel(place_ref, a_ref, b_ref, c_ref, d_ref, dir_ref, new_ref, weights_hbm, dir_hbm, new_hbm, staged, sems):
    copies = [
        pltpu.make_async_copy(dir_ref, dir_hbm, sems.at[CHUNKS]),
        pltpu.make_async_copy(new_ref, new_hbm, sems.at[CHUNKS + 1]),
    ]
    for copy in copies:
        copy.start()
    half = place_ref[0] // 16 % 2
    for copy in copies + place_half(place_ref[0], half, (a_ref, b_ref, c_ref, d_ref), weights_hbm, staged, sems):
        copy.wait()


def restore_own(place, blocks, adam_dir, new_master):
    slab = jax.ShapeDtypeStruct((1, HALF), F32)
    return pl.pallas_call(
        restore_own_kernel,
        out_shape=(jax.ShapeDtypeStruct((ROWS, WIDTH), BF16), slab, slab),
        in_specs=[SCALAR] + [WHOLE] * 6,
        out_specs=[FAR] * 3,
        scratch_shapes=[pltpu.VMEM((CHUNKS, ROWS, CHUNK), BF16), pltpu.SemaphoreType.DMA((CHUNKS + 2,))],
        compiler_params=params(),
        name="restore_own",
    )(place, *blocks, adam_dir, new_master)


def restore_other_kernel(place_ref, a_ref, b_ref, c_ref, d_ref, held_hbm, weights_hbm, staged, sems):
    half = 1 - place_ref[0] // 16 % 2
    for copy in place_half(place_ref[0], half, (a_ref, b_ref, c_ref, d_ref), weights_hbm, staged, sems):
        copy.wait()


def restore_other(place, blocks, weights):
    return pl.pallas_call(
        restore_other_kernel,
        out_shape=jax.ShapeDtypeStruct((ROWS, WIDTH), BF16),
        in_specs=[SCALAR] + [WHOLE] * 4 + [FAR],
        out_specs=FAR,
        scratch_shapes=[pltpu.VMEM((CHUNKS, ROWS, CHUNK), BF16), pltpu.SemaphoreType.DMA((CHUNKS,))],
        input_output_aliases={5: 0},
        compiler_params=params(),
        name="restore_other",
    )(place, *blocks, weights)


def shards(grad_codes, scales, feedback, master, moment, second):
    place = lax.axis_index(AXES).astype(jnp.int32).reshape(1)
    codes, feed = grad_codes[0, 0], feedback[0, 0]
    turned = jnp.swapaxes(scales[0, 0], 0, 1)
    *given, kept = compensate(place, codes, turned, feed)
    taken = {piece: swap_cores(given[piece]) for piece in (2, 1, 3, 0)}
    sums = {piece: pair_sum(piece, kept, taken[piece]) for piece in (2, 1, 3, 0)}
    partial = line_sum(sums[0], [send(sums[step], step) for step in (2, 1, 3)])
    arrived = exchange(partial.reshape(32, *SLAB), owner_groups())
    adam_dir, new_master, copies = adam(arrived, master[0], moment[0], second[0])
    joined = exchange(copies, owner_groups()).reshape(32, HALF)
    mine = [joined] + [send(joined, step) for step in (3, 1, 2)]
    theirs = [swap_cores(block) for block in mine]
    weights, adam_dir, new_master = restore_own(place, mine, adam_dir, new_master)
    weights = restore_other(place, theirs, weights)
    return adam_dir[None], new_master[None], weights


def solution(mesh):
    fine = Mesh(mesh.devices.reshape(SIZES), AXES)
    wide, node = ("y", "zh", "core"), ("zl", "x")
    placed = (
        P(wide, node, None, None),
        P(wide, node, None, None),
        P(wide, node, None, None),
        P(node, wide, None),
        P(node, wide, None),
        P(node, wide, None),
    )
    return jax.shard_map(
        shards,
        mesh=fine,
        in_specs=placed,
        out_specs=(P(node, wide, None), P(node, wide, None), P()),
        check_vma=False,
    )
```

```python
import functools

import jax
import jax.numpy as jnp
from jax import lax
from jax.experimental import pallas as pl
from jax.experimental.pallas import tpu as pltpu
from jax.sharding import Mesh
from jax.sharding import PartitionSpec as P

beta_one = 0.9
beta_two = 0.999
adam_count = 100.0
adam_epsilon = 1e-08
learn_rate = 0.02

AXES = ("y", "zh", "core", "zl", "x")
SIZES = (4, 2, 2, 4, 4)
ROWS = 128
WIDTH = 9216
HALF = WIDTH // 2
LANES = 128
CHUNKS = 3
CHUNK = HALF // CHUNKS
PER_CHUNK = CHUNK // LANES
SLAB_ROWS = HALF // LANES
SLAB = (2, HALF // 2)
F32 = jnp.float32
BF16 = jnp.bfloat16
VMEM_LIMIT = 32 * 1024 * 1024
WHOLE = pl.BlockSpec(memory_space=pltpu.VMEM)
SCALAR = pl.BlockSpec(memory_space=pltpu.SMEM)
FAR = pl.BlockSpec(memory_space=pltpu.HBM)


def params():
    return pltpu.CompilerParams(vmem_limit_bytes=VMEM_LIMIT)


def in_hbm(array):
    return pltpu.with_memory_space_constraint(array, pltpu.HBM)


def device(x, y, z, core):
    return (((y * 2 + z // 4) * 2 + core) * 4 + z % 4) * 4 + x


def owner_groups():
    lines = [(zl + 4 * zh) for zl in range(4) for zh in range(2)]
    groups = [[device(x, y, z, 0) for y in range(4) for z in lines] for x in range(4)]
    return groups + [[device(x, y, z, 1) for x in range(4) for z in lines] for y in range(4)]


def shifted(step):
    pairs = []
    for i in range(256):
        x, zl, core, zh, y = i % 4, i // 4 % 4, i // 16 % 2, i // 32 % 2, i // 64
        z = zl + 4 * zh
        pairs.append((i, device(x, (y + step) % 4, z, 1) if core else device((x + step) % 4, y, z, 0)))
    return pairs


SWAP = [(i, i ^ 16) for i in range(256)]


def swap_cores(array):
    return lax.ppermute(array, AXES, SWAP)


def send(array, step):
    return lax.ppermute(array, AXES, shifted(step))


def exchange(array, groups):
    return lax.all_to_all(array, AXES, 0, 0, axis_index_groups=groups, tiled=True)


def order(place, half, transposed):
    sent = lax.broadcasted_iota(jnp.int32, (ROWS, ROWS), 1 if transposed else 0)
    flat = lax.broadcasted_iota(jnp.int32, (ROWS, ROWS), 0 if transposed else 1)
    own, a_step = jnp.where(half == 0, place % 4, place // 64), jnp.where(half == 0, 8, 2)
    a, b = (sent // 32 + own) % 4, sent // 8 % 4
    return (sent // 2 % 4 * 32 + a * a_step + b * (10 - a_step) + sent % 2 == flat).astype(F32).astype(BF16)


def compensate_kernel(place_ref, codes_hbm, scales_hbm, feedback_hbm, *refs):
    *given_refs, kept_ref, codes, scales, feedback, turned, summed, sems = refs
    core = place_ref[0] // 16 % 2
    copies = [pltpu.make_async_copy(scales_hbm, scales, sems.at[4 * CHUNKS])]
    for turn in range(2):
        start = (core if turn else 1 - core) * HALF
        for i in range(CHUNKS):
            columns = pl.ds(pl.multiple_of(start + i * CHUNK, LANES), CHUNK)
            at = turn * CHUNKS + i
            copies.append(pltpu.make_async_copy(codes_hbm.at[:, columns], codes.at[at], sems.at[2 * at]))
            copies.append(pltpu.make_async_copy(feedback_hbm.at[:, columns], feedback.at[at], sems.at[2 * at + 1]))
    for copy in copies:
        copy.start()
    moved = order(place_ref[0], 1 - core, False)
    copies[0].wait()
    for turn in range(2):
        half = core if turn else 1 - core
        turned[turn, 0:SLAB_ROWS, :] = scales[pl.ds(half * SLAB_ROWS, SLAB_ROWS), :]
        scale = turned[turn].T
        for i in range(CHUNKS):
            at = turn * CHUNKS + i
            copies[1 + 2 * at].wait()
            copies[2 + 2 * at].wait()
            for block in range(PER_CHUNK):
                columns = slice(block * LANES, (block + 1) * LANES)
                place = i * PER_CHUNK + block
                dequant = codes[at, :, columns].astype(F32) * scale[:, place : place + 1]
                into = slice(place * LANES, (place + 1) * LANES)
                held = kept_ref if turn else summed
                held[:, into] = (dequant + feedback[at, :, columns].astype(F32)).astype(BF16)
        if turn == 0:
            for i in range(CHUNKS):
                columns = slice(i * CHUNK, (i + 1) * CHUNK)
                rows = jnp.dot(moved, summed[:, columns], preferred_element_type=F32).astype(BF16)
                for piece, given_ref in enumerate(given_refs):
                    given_ref[:, columns] = rows[piece * 32 : (piece + 1) * 32]


def compensate(place, codes, scales, feedback):
    return pl.pallas_call(
        compensate_kernel,
        out_shape=[jax.ShapeDtypeStruct((32, HALF), BF16)] * 4 + [jax.ShapeDtypeStruct((ROWS, HALF), BF16)],
        in_specs=[SCALAR, FAR, FAR, FAR],
        out_specs=[WHOLE] * 5,
        scratch_shapes=[
            pltpu.VMEM((2 * CHUNKS, ROWS, CHUNK), jnp.int32),
            pltpu.VMEM((WIDTH // LANES, ROWS), F32),
            pltpu.VMEM((2 * CHUNKS, ROWS, CHUNK), BF16),
            pltpu.VMEM((2, ROWS, LANES), F32),
            pltpu.VMEM((ROWS, HALF), BF16),
            pltpu.SemaphoreType.DMA((4 * CHUNKS + 1,)),
        ],
        compiler_params=params(),
        name="compensate",
    )(place, in_hbm(codes), in_hbm(scales), in_hbm(feedback))


def put_in_order_kernel(place_ref, in_ref, out_ref):
    moved = order(place_ref[0], place_ref[0] // 16 % 2, False)
    for i in range(CHUNKS):
        columns = slice(i * CHUNK, (i + 1) * CHUNK)
        out_ref[:, columns] = jnp.dot(moved, in_ref[:, columns], preferred_element_type=F32).astype(BF16)


def put_in_order(place, rows):
    return pl.pallas_call(
        put_in_order_kernel,
        out_shape=jax.ShapeDtypeStruct((ROWS, HALF), BF16),
        in_specs=[SCALAR, WHOLE],
        out_specs=WHOLE,
        compiler_params=params(),
        name="put_in_order",
    )(place, rows)


def pair_sum_kernel(piece, own_ref, other_ref, out_ref):
    own = own_ref[piece * 32 : (piece + 1) * 32, :].astype(F32)
    out_ref[...] = (own + other_ref[...].astype(F32)).astype(BF16)


def pair_sum(piece, own, other):
    return pl.pallas_call(
        functools.partial(pair_sum_kernel, piece),
        out_shape=jax.ShapeDtypeStruct((32, HALF), BF16),
        in_specs=[WHOLE] * 2,
        out_specs=WHOLE,
        compiler_params=params(),
        name="pair_sum",
    )(own, other)


def line_sum_kernel(own_ref, a_ref, b_ref, c_ref, out_ref):
    total = own_ref[...].astype(F32) + a_ref[...].astype(F32) + b_ref[...].astype(F32) + c_ref[...].astype(F32)
    out_ref[...] = total.astype(BF16)


def line_sum(own, arrived):
    return pl.pallas_call(
        line_sum_kernel,
        out_shape=jax.ShapeDtypeStruct((32, HALF), BF16),
        in_specs=[WHOLE] * 4,
        out_specs=WHOLE,
        compiler_params=params(),
        name="line_sum",
    )(own, *arrived)


def adam_kernel(arrived_ref, master_ref, moment_ref, second_ref, dir_ref, new_ref, copies_ref):
    total = arrived_ref[0].astype(F32)
    for piece in range(1, 32):
        total = total + arrived_ref[piece].astype(F32)
    grad = jnp.concatenate([total[0:1], total[1:2]], axis=1) / 256.0
    first = beta_one * moment_ref[...] + (1.0 - beta_one) * grad
    squared = beta_two * second_ref[...] + (1.0 - beta_two) * grad * grad
    first_hat = first / (1.0 - beta_one**adam_count)
    squared_hat = squared / (1.0 - beta_two**adam_count)
    adam_dir = first_hat / (jnp.sqrt(squared_hat) + adam_epsilon)
    new_master = master_ref[...] - learn_rate * adam_dir
    dir_ref[...] = adam_dir
    new_ref[...] = new_master
    rows = jnp.concatenate([new_master[:, : SLAB[1]], new_master[:, SLAB[1] :]], axis=0)
    copies_ref[...] = jnp.broadcast_to(rows.astype(BF16)[None], copies_ref.shape)


def adam(arrived, master, moment, second):
    slab = jax.ShapeDtypeStruct((1, HALF), F32)
    return pl.pallas_call(
        adam_kernel,
        out_shape=(slab, slab, jax.ShapeDtypeStruct((32, *SLAB), BF16)),
        in_specs=[WHOLE] * 4,
        out_specs=[WHOLE] * 3,
        compiler_params=params(),
        name="adam",
    )(arrived, master, moment, second)


def place_half(place, half, blocks, weights_hbm, staged, sems):
    moved = order(place, half, True)
    ordered = [blocks[i] for i in (0, 1, 3, 2)]
    copies = []
    for i in range(CHUNKS):
        rows = jnp.concatenate([block[:, i * CHUNK : (i + 1) * CHUNK] for block in ordered], axis=0)
        staged[i] = jnp.dot(moved, rows, preferred_element_type=F32).astype(BF16)
        to = pl.ds(pl.multiple_of(half * HALF + i * CHUNK, LANES), CHUNK)
        copies.append(pltpu.make_async_copy(staged.at[i], weights_hbm.at[:, to], sems.at[i]))
        copies[-1].start()
    return copies


def restore_own_kernel(place_ref, a_ref, b_ref, c_ref, d_ref, dir_ref, new_ref, weights_hbm, dir_hbm, new_hbm, staged, sems):
    copies = [
        pltpu.make_async_copy(dir_ref, dir_hbm, sems.at[CHUNKS]),
        pltpu.make_async_copy(new_ref, new_hbm, sems.at[CHUNKS + 1]),
    ]
    for copy in copies:
        copy.start()
    half = place_ref[0] // 16 % 2
    for copy in copies + place_half(place_ref[0], half, (a_ref, b_ref, c_ref, d_ref), weights_hbm, staged, sems):
        copy.wait()


def restore_own(place, blocks, adam_dir, new_master):
    slab = jax.ShapeDtypeStruct((1, HALF), F32)
    return pl.pallas_call(
        restore_own_kernel,
        out_shape=(jax.ShapeDtypeStruct((ROWS, WIDTH), BF16), slab, slab),
        in_specs=[SCALAR] + [WHOLE] * 6,
        out_specs=[FAR] * 3,
        scratch_shapes=[pltpu.VMEM((CHUNKS, ROWS, CHUNK), BF16), pltpu.SemaphoreType.DMA((CHUNKS + 2,))],
        compiler_params=params(),
        name="restore_own",
    )(place, *blocks, adam_dir, new_master)


def restore_other_kernel(place_ref, a_ref, b_ref, c_ref, d_ref, held_hbm, weights_hbm, staged, sems):
    half = 1 - place_ref[0] // 16 % 2
    for copy in place_half(place_ref[0], half, (a_ref, b_ref, c_ref, d_ref), weights_hbm, staged, sems):
        copy.wait()


def restore_other(place, blocks, weights):
    return pl.pallas_call(
        restore_other_kernel,
        out_shape=jax.ShapeDtypeStruct((ROWS, WIDTH), BF16),
        in_specs=[SCALAR] + [WHOLE] * 4 + [FAR],
        out_specs=FAR,
        scratch_shapes=[pltpu.VMEM((CHUNKS, ROWS, CHUNK), BF16), pltpu.SemaphoreType.DMA((CHUNKS,))],
        input_output_aliases={5: 0},
        compiler_params=params(),
        name="restore_other",
    )(place, *blocks, weights)


def shards(grad_codes, scales, feedback, master, moment, second):
    place = lax.axis_index(AXES).astype(jnp.int32).reshape(1)
    codes, feed = grad_codes[0, 0], feedback[0, 0]
    turned = jnp.swapaxes(scales[0, 0], 0, 1)
    *given, kept = compensate(place, codes, turned, feed)
    taken = {piece: swap_cores(given[piece]) for piece in (2, 1, 3, 0)}
    kept = put_in_order(place, kept)
    sums = {piece: pair_sum(piece, kept, taken[piece]) for piece in (2, 1, 3, 0)}
    partial = line_sum(sums[0], [send(sums[step], step) for step in (2, 1, 3)])
    arrived = exchange(partial.reshape(32, *SLAB), owner_groups())
    adam_dir, new_master, copies = adam(arrived, master[0], moment[0], second[0])
    joined = exchange(copies, owner_groups()).reshape(32, HALF)
    mine = [joined] + [send(joined, step) for step in (3, 1, 2)]
    theirs = [swap_cores(block) for block in mine]
    weights, adam_dir, new_master = restore_own(place, mine, adam_dir, new_master)
    weights = restore_other(place, theirs, weights)
    return adam_dir[None], new_master[None], weights


def solution(mesh):
    fine = Mesh(mesh.devices.reshape(SIZES), AXES)
    wide, node = ("y", "zh", "core"), ("zl", "x")
    placed = (
        P(wide, node, None, None),
        P(wide, node, None, None),
        P(wide, node, None, None),
        P(node, wide, None),
        P(node, wide, None),
        P(node, wide, None),
    )
    return jax.shard_map(
        shards,
        mesh=fine,
        in_specs=placed,
        out_specs=(P(node, wide, None), P(node, wide, None), P()),
        check_vma=False,
    )
```

```python
import functools

import jax
import jax.numpy as jnp
from jax import lax
from jax.experimental import pallas as pl
from jax.experimental.pallas import tpu as pltpu
from jax.sharding import Mesh
from jax.sharding import PartitionSpec as P

beta_one = 0.9
beta_two = 0.999
adam_count = 100.0
adam_epsilon = 1e-08
learn_rate = 0.02

AXES = ("y", "zh", "core", "zl", "x")
SIZES = (4, 2, 2, 4, 4)
ROWS = 128
WIDTH = 9216
HALF = WIDTH // 2
LANES = 128
CHUNKS = 3
CHUNK = HALF // CHUNKS
PER_CHUNK = CHUNK // LANES
SLAB_ROWS = HALF // LANES
SLAB = (2, HALF // 2)
F32 = jnp.float32
BF16 = jnp.bfloat16
VMEM_LIMIT = 32 * 1024 * 1024
WHOLE = pl.BlockSpec(memory_space=pltpu.VMEM)
SCALAR = pl.BlockSpec(memory_space=pltpu.SMEM)
FAR = pl.BlockSpec(memory_space=pltpu.HBM)


def params():
    return pltpu.CompilerParams(vmem_limit_bytes=VMEM_LIMIT)


def in_hbm(array):
    return pltpu.with_memory_space_constraint(array, pltpu.HBM)


def device(x, y, z, core):
    return (((y * 2 + z // 4) * 2 + core) * 4 + z % 4) * 4 + x


def owner_groups():
    lines = [(zl + 4 * zh) for zl in range(4) for zh in range(2)]
    groups = [[device(x, y, z, 0) for y in range(4) for z in lines] for x in range(4)]
    return groups + [[device(x, y, z, 1) for x in range(4) for z in lines] for y in range(4)]


def shifted(step):
    pairs = []
    for i in range(256):
        x, zl, core, zh, y = i % 4, i // 4 % 4, i // 16 % 2, i // 32 % 2, i // 64
        z = zl + 4 * zh
        pairs.append((i, device(x, (y + step) % 4, z, 1) if core else device((x + step) % 4, y, z, 0)))
    return pairs


SWAP = [(i, i ^ 16) for i in range(256)]


def swap_cores(array):
    return lax.ppermute(array, AXES, SWAP)


def send(array, step):
    return lax.ppermute(array, AXES, shifted(step))


def exchange(array, groups):
    return lax.all_to_all(array, AXES, 0, 0, axis_index_groups=groups, tiled=True)


def order(place, half, transposed):
    sent = lax.broadcasted_iota(jnp.int32, (ROWS, ROWS), 1 if transposed else 0)
    flat = lax.broadcasted_iota(jnp.int32, (ROWS, ROWS), 0 if transposed else 1)
    own, a_step = jnp.where(half == 0, place % 4, place // 64), jnp.where(half == 0, 8, 2)
    a, b = (sent // 32 + own) % 4, sent // 8 % 4
    return (sent // 2 % 4 * 32 + a * a_step + b * (10 - a_step) + sent % 2 == flat).astype(F32).astype(BF16)


def compensate_kernel(place_ref, codes_hbm, scales_hbm, feedback_hbm, *refs):
    *given_refs, kept_ref, codes, scales, feedback, turned, summed, sems = refs
    core = place_ref[0] // 16 % 2
    copies = [pltpu.make_async_copy(scales_hbm, scales, sems.at[4 * CHUNKS])]
    for turn in range(2):
        start = (core if turn else 1 - core) * HALF
        for i in range(CHUNKS):
            columns = pl.ds(pl.multiple_of(start + i * CHUNK, LANES), CHUNK)
            at = turn * CHUNKS + i
            copies.append(pltpu.make_async_copy(codes_hbm.at[:, columns], codes.at[at], sems.at[2 * at]))
            copies.append(pltpu.make_async_copy(feedback_hbm.at[:, columns], feedback.at[at], sems.at[2 * at + 1]))
    for copy in copies:
        copy.start()
    moved = order(place_ref[0], 1 - core, False)
    copies[0].wait()
    for turn in range(2):
        half = core if turn else 1 - core
        turned[turn, 0:SLAB_ROWS, :] = scales[pl.ds(half * SLAB_ROWS, SLAB_ROWS), :]
        scale = turned[turn].T
        for i in range(CHUNKS):
            at = turn * CHUNKS + i
            copies[1 + 2 * at].wait()
            copies[2 + 2 * at].wait()
            for block in range(PER_CHUNK):
                columns = slice(block * LANES, (block + 1) * LANES)
                place = i * PER_CHUNK + block
                dequant = codes[at, :, columns].astype(F32) * scale[:, place : place + 1]
                into = slice(place * LANES, (place + 1) * LANES)
                held = kept_ref if turn else summed
                held[:, into] = (dequant + feedback[at, :, columns].astype(F32)).astype(BF16)
        if turn == 0:
            for i in range(CHUNKS):
                columns = slice(i * CHUNK, (i + 1) * CHUNK)
                rows = jnp.dot(moved, summed[:, columns], preferred_element_type=F32).astype(BF16)
                far_ref, near_ref = given_refs
                far_ref[:, columns] = rows[64:96]
                near_ref[0:64, columns] = rows[0:64]
                near_ref[64:96, columns] = rows[96:128]


def compensate(place, codes, scales, feedback):
    return pl.pallas_call(
        compensate_kernel,
        out_shape=[jax.ShapeDtypeStruct((rows, HALF), BF16) for rows in (32, 96, ROWS)],
        in_specs=[SCALAR, FAR, FAR, FAR],
        out_specs=[WHOLE] * 3,
        scratch_shapes=[
            pltpu.VMEM((2 * CHUNKS, ROWS, CHUNK), jnp.int32),
            pltpu.VMEM((WIDTH // LANES, ROWS), F32),
            pltpu.VMEM((2 * CHUNKS, ROWS, CHUNK), BF16),
            pltpu.VMEM((2, ROWS, LANES), F32),
            pltpu.VMEM((ROWS, HALF), BF16),
            pltpu.SemaphoreType.DMA((4 * CHUNKS + 1,)),
        ],
        compiler_params=params(),
        name="compensate",
    )(place, in_hbm(codes), in_hbm(scales), in_hbm(feedback))


def put_in_order_kernel(place_ref, in_ref, out_ref):
    moved = order(place_ref[0], place_ref[0] // 16 % 2, False)
    for i in range(CHUNKS):
        columns = slice(i * CHUNK, (i + 1) * CHUNK)
        out_ref[:, columns] = jnp.dot(moved, in_ref[:, columns], preferred_element_type=F32).astype(BF16)


def put_in_order(place, rows):
    return pl.pallas_call(
        put_in_order_kernel,
        out_shape=jax.ShapeDtypeStruct((ROWS, HALF), BF16),
        in_specs=[SCALAR, WHOLE],
        out_specs=WHOLE,
        compiler_params=params(),
        name="put_in_order",
    )(place, rows)


def pair_sum_kernel(piece, own_ref, other_ref, out_ref):
    own = own_ref[piece * 32 : (piece + 1) * 32, :].astype(F32)
    low = (0, 32, 0, 64)[piece]
    out_ref[...] = (own + other_ref[low : low + 32, :].astype(F32)).astype(BF16)


def pair_sum(piece, own, other):
    return pl.pallas_call(
        functools.partial(pair_sum_kernel, piece),
        out_shape=jax.ShapeDtypeStruct((32, HALF), BF16),
        in_specs=[WHOLE] * 2,
        out_specs=WHOLE,
        compiler_params=params(),
        name="pair_sum",
    )(own, other)


def line_sum_kernel(own_ref, a_ref, b_ref, c_ref, out_ref):
    total = own_ref[...].astype(F32) + a_ref[...].astype(F32) + b_ref[...].astype(F32) + c_ref[...].astype(F32)
    out_ref[...] = total.astype(BF16)


def line_sum(own, arrived):
    return pl.pallas_call(
        line_sum_kernel,
        out_shape=jax.ShapeDtypeStruct((32, HALF), BF16),
        in_specs=[WHOLE] * 4,
        out_specs=WHOLE,
        compiler_params=params(),
        name="line_sum",
    )(own, *arrived)


def adam_kernel(arrived_ref, master_ref, moment_ref, second_ref, dir_ref, new_ref, copies_ref):
    total = arrived_ref[0].astype(F32)
    for piece in range(1, 32):
        total = total + arrived_ref[piece].astype(F32)
    grad = jnp.concatenate([total[0:1], total[1:2]], axis=1) / 256.0
    first = beta_one * moment_ref[...] + (1.0 - beta_one) * grad
    squared = beta_two * second_ref[...] + (1.0 - beta_two) * grad * grad
    first_hat = first / (1.0 - beta_one**adam_count)
    squared_hat = squared / (1.0 - beta_two**adam_count)
    adam_dir = first_hat / (jnp.sqrt(squared_hat) + adam_epsilon)
    new_master = master_ref[...] - learn_rate * adam_dir
    dir_ref[...] = adam_dir
    new_ref[...] = new_master
    rows = jnp.concatenate([new_master[:, : SLAB[1]], new_master[:, SLAB[1] :]], axis=0)
    copies_ref[...] = jnp.broadcast_to(rows.astype(BF16)[None], copies_ref.shape)


def adam(arrived, master, moment, second):
    slab = jax.ShapeDtypeStruct((1, HALF), F32)
    return pl.pallas_call(
        adam_kernel,
        out_shape=(slab, slab, jax.ShapeDtypeStruct((32, *SLAB), BF16)),
        in_specs=[WHOLE] * 4,
        out_specs=[WHOLE] * 3,
        compiler_params=params(),
        name="adam",
    )(arrived, master, moment, second)


def place_half(place, half, blocks, weights_hbm, staged, sems):
    moved = order(place, half, True)
    ordered = [blocks[i] for i in (0, 1, 3, 2)]
    copies = []
    for i in range(CHUNKS):
        rows = jnp.concatenate([block[:, i * CHUNK : (i + 1) * CHUNK] for block in ordered], axis=0)
        staged[i] = jnp.dot(moved, rows, preferred_element_type=F32).astype(BF16)
        to = pl.ds(pl.multiple_of(half * HALF + i * CHUNK, LANES), CHUNK)
        copies.append(pltpu.make_async_copy(staged.at[i], weights_hbm.at[:, to], sems.at[i]))
        copies[-1].start()
    return copies


def restore_own_kernel(place_ref, a_ref, b_ref, c_ref, d_ref, dir_ref, new_ref, weights_hbm, dir_hbm, new_hbm, staged, sems):
    copies = [
        pltpu.make_async_copy(dir_ref, dir_hbm, sems.at[CHUNKS]),
        pltpu.make_async_copy(new_ref, new_hbm, sems.at[CHUNKS + 1]),
    ]
    for copy in copies:
        copy.start()
    half = place_ref[0] // 16 % 2
    for copy in copies + place_half(place_ref[0], half, (a_ref, b_ref, c_ref, d_ref), weights_hbm, staged, sems):
        copy.wait()


def restore_own(place, blocks, adam_dir, new_master):
    slab = jax.ShapeDtypeStruct((1, HALF), F32)
    return pl.pallas_call(
        restore_own_kernel,
        out_shape=(jax.ShapeDtypeStruct((ROWS, WIDTH), BF16), slab, slab),
        in_specs=[SCALAR] + [WHOLE] * 6,
        out_specs=[FAR] * 3,
        scratch_shapes=[pltpu.VMEM((CHUNKS, ROWS, CHUNK), BF16), pltpu.SemaphoreType.DMA((CHUNKS + 2,))],
        compiler_params=params(),
        name="restore_own",
    )(place, *blocks, adam_dir, new_master)


def restore_other_kernel(place_ref, a_ref, b_ref, c_ref, d_ref, held_hbm, weights_hbm, staged, sems):
    half = 1 - place_ref[0] // 16 % 2
    for copy in place_half(place_ref[0], half, (a_ref, b_ref, c_ref, d_ref), weights_hbm, staged, sems):
        copy.wait()


def restore_other(place, blocks, weights):
    return pl.pallas_call(
        restore_other_kernel,
        out_shape=jax.ShapeDtypeStruct((ROWS, WIDTH), BF16),
        in_specs=[SCALAR] + [WHOLE] * 4 + [FAR],
        out_specs=FAR,
        scratch_shapes=[pltpu.VMEM((CHUNKS, ROWS, CHUNK), BF16), pltpu.SemaphoreType.DMA((CHUNKS,))],
        input_output_aliases={5: 0},
        compiler_params=params(),
        name="restore_other",
    )(place, *blocks, weights)


def shards(grad_codes, scales, feedback, master, moment, second):
    place = lax.axis_index(AXES).astype(jnp.int32).reshape(1)
    codes, feed = grad_codes[0, 0], feedback[0, 0]
    turned = jnp.swapaxes(scales[0, 0], 0, 1)
    far, near, kept = compensate(place, codes, turned, feed)
    far, near = swap_cores(far), swap_cores(near)
    taken = (near, near, far, near)
    kept = put_in_order(place, kept)
    sums = {piece: pair_sum(piece, kept, taken[piece]) for piece in (2, 1, 3, 0)}
    partial = line_sum(sums[0], [send(sums[step], step) for step in (2, 1, 3)])
    arrived = exchange(partial.reshape(32, *SLAB), owner_groups())
    adam_dir, new_master, copies = adam(arrived, master[0], moment[0], second[0])
    joined = exchange(copies, owner_groups()).reshape(32, HALF)
    mine = [joined] + [send(joined, step) for step in (3, 1, 2)]
    theirs = [swap_cores(block) for block in mine]
    weights, adam_dir, new_master = restore_own(place, mine, adam_dir, new_master)
    weights = restore_other(place, theirs, weights)
    return adam_dir[None], new_master[None], weights


def solution(mesh):
    fine = Mesh(mesh.devices.reshape(SIZES), AXES)
    wide, node = ("y", "zh", "core"), ("zl", "x")
    placed = (
        P(wide, node, None, None),
        P(wide, node, None, None),
        P(wide, node, None, None),
        P(node, wide, None),
        P(node, wide, None),
        P(node, wide, None),
    )
    return jax.shard_map(
        shards,
        mesh=fine,
        in_specs=placed,
        out_specs=(P(node, wide, None), P(node, wide, None), P()),
        check_vma=False,
    )
```
